128 devices in a mesh: dp: 2 (over x_lo), ctx: 64 (over y, z, x_hi, core).
Axes of the slice: x: 4 (x_hi: 2, x_lo: 2; x = x_hi * 2 + x_lo), y: 4, z: 4, core: 2. Of those that a mesh axis runs over, the one named last changes fastest.
Arguments:
- saved_input: bfloat16 [2, 32768, 512], P('dp', 'ctx'), may hold values from -6 to 6
- output_grad: bfloat16 [2, 32768, 512], P('dp', 'ctx'), may hold values from -0.0625 to 0.0625
- filter_taps: bfloat16 [32768, 512], P('ctx'), may hold values from -6 to 6
Outputs:
- input_grad: bfloat16 [2, 32768, 512], P('dp', 'ctx')
- filter_grad: float32 [32768, 512], P('ctx', 'dp')
The draws below stay inside these ranges and needn't reach their ends.
All inputs are finite; a program needn't handle non-finite values.
Results may differ from the reference program's by a relative error of at most 0.001.
Values may be sent and summed in bfloat16 or wider, within the bound.
No kernel may reach another device: no remote copies, remote signals or barrier semaphores. Data moves between devices by JAX's collectives and lax.ppermute only.
A program may use at most 128 MiB of HBM per device.

```python
import jax
import jax.numpy as jnp

CH = 512
SEQ = 32768
BATCH = 2


def level_of(rng, extent, cuts, smallest, top_value):
    factor_of, own = 1.0, jax.random.fold_in(rng, 6)
    for position, parts in cuts:
        steps = jnp.exp(jax.random.uniform(jax.random.fold_in(own, position), (parts,), jnp.float32, smallest / len(cuts), top_value / len(cuts)))
        factor_of = factor_of * jnp.repeat(steps, extent[position] // parts).reshape([-1 if axis == position else 1 for axis in range(len(extent))])
    return factor_of


def noise(stream_key, shape, scale, limit, cuts=(), held_as=jnp.bfloat16):
    entries = jax.random.normal(stream_key, shape, jnp.float32) * scale
    if len(cuts) > 0:
        entries = level_of(stream_key, shape, cuts, -0.22, 0.18) * entries
    return jnp.clip(entries, min=-limit, max=limit).astype(held_as)


def setup_inputs(seed: int = 0) -> dict:
    key_of = jax.random.split(jax.random.key(seed), 4)
    return {
        "saved_input": noise(key_of[0], (BATCH, SEQ, CH), 1.0, 6.0, ((0, 2), (1, 64))),
        "output_grad": noise(key_of[1], (BATCH, SEQ, CH), ((2 * SEQ) ** -0.5), 0.0625, ((0, 2), (1, 64))),
        "filter_taps": noise(key_of[2], (SEQ, CH), 1.0, 6.0, ((0, 64),)),
    }


def reference(saved_input, output_grad, filter_taps):
    fft_length = 2 * SEQ
    signal_spec = jnp.fft.rfft(saved_input.astype(jnp.float32), n=fft_length, axis=1)
    grad_spec = jnp.fft.rfft(output_grad.astype(jnp.float32), n=fft_length, axis=1)
    filter_spec = jnp.fft.rfft(filter_taps.astype(jnp.float32), n=fft_length, axis=0)
    input_prod = grad_spec * jnp.conj(filter_spec)[None]
    filter_prod = jnp.sum(grad_spec * jnp.conj(signal_spec), axis=0)
    input_grad = jnp.fft.irfft(input_prod, n=fft_length, axis=1)[:, :SEQ]
    filter_grad = jnp.fft.irfft(filter_prod, n=fft_length, axis=0)[:SEQ]
    return input_grad.astype(jnp.bfloat16), filter_grad.astype(jnp.float32)
```

```python
import functools
import math

import jax
import jax.numpy as jnp
import ml_dtypes
import numpy as np
from jax import lax
from jax.experimental import pallas as pl
from jax.experimental.pallas import tpu as pltpu
from jax.sharding import PartitionSpec as P

LANES = 128
BF16 = jnp.bfloat16
F32 = jnp.float32
OWN = 4
BATCH = 2


def two_parts(matrix):
    high = matrix.astype(ml_dtypes.bfloat16)
    low = (matrix - high.astype(np.float64)).astype(ml_dtypes.bfloat16)
    return high, low


def turn(numerator, period):
    phase = (numerator % period) * (2.0 * math.pi / period)
    return np.cos(phase), np.sin(phase)


@functools.cache
def tables(seq):
    rows = seq // LANES
    k1 = np.arange(rows, dtype=np.int64)[:, None]
    a = np.arange(rows, dtype=np.int64)[None, :]
    r = np.arange(LANES, dtype=np.int64)
    cos_a, sin_a = turn((4 * k1 + 1) * a, 4 * rows)
    first = np.concatenate([cos_a, -sin_a], axis=0)
    last = np.concatenate([cos_a.T, -sin_a.T], axis=1) / seq
    cos_t, sin_t = turn((4 * k1 + 1) * r[None, :], 4 * seq)
    cos_r, sin_r = turn(r[:, None] * r[None, :], LANES)
    forth = np.block([[cos_r, -sin_r], [sin_r, cos_r]])
    back = np.block([[cos_r, sin_r], [-sin_r, cos_r]])
    return (
        np.concatenate(two_parts(first), axis=0),
        np.concatenate(two_parts(last), axis=0),
        np.concatenate(two_parts(forth), axis=0),
        np.concatenate(two_parts(back), axis=0),
        np.concatenate([cos_t, sin_t], axis=0).astype(np.float32),
    )


def dot(left, right):
    return jnp.dot(left, right, preferred_element_type=F32)


def split(value):
    high = value.astype(BF16)
    return high, (value - high.astype(F32)).astype(BF16)


def pack_kernel(peers, dp_index, u_ref, g_ref, h_ref, out_ref, held):
    blocks = u_ref.shape[0] // LANES
    group = peers // 2

    def place(ref, block, row):
        flipped = ref[block * LANES : (block + 1) * LANES, :].astype(F32).T
        for c in range(OWN):
            held[pl.ds(row + c, peers, stride=40), :] = flipped[c * peers : (c + 1) * peers, :]

    for q in range(blocks):
        place(u_ref, q, OWN * q)
        place(g_ref, q, 16 + OWN * q)
    for q in range(2):
        place(h_ref, q, 32 + OWN * q)
    out_ref[...] = held[...].reshape(peers, 40, LANES).astype(BF16)


def unpack_kernel(peers, in_ref, input_ref, filter_ref, held):
    blocks = input_ref.shape[0] // LANES
    held[...] = in_ref[...].astype(F32).reshape(peers * 32, LANES)
    for q in range(blocks):
        rows = slice(q * LANES, (q + 1) * LANES)
        for c in range(OWN):
            piece = held[pl.ds(OWN * q + c, peers, stride=32), :]
            input_ref[rows, c * peers : (c + 1) * peers] = piece.T.astype(BF16)
        for c in range(OWN // 2):
            high = held[pl.ds(16 + 2 * q + c, peers, stride=32), :]
            low = held[pl.ds(24 + 2 * q + c, peers, stride=32), :]
            filter_ref[rows, c * peers : (c + 1) * peers] = (high + low).T


def convolve_kernel(group, in_ref, first_ref, last_ref, forth_ref, back_ref, turn_ref, out_ref, u_held, g_held, h_held, in_grad, taps_grad):
    rows = group * OWN
    for b in range(BATCH):
        got = in_ref[b * group : (b + 1) * group].astype(F32)
        u_held[b] = got[:, 0:16].reshape(group * 16, LANES)
        g_held[b] = got[:, 16:32].reshape(group * 16, LANES)
    taps = [in_ref[b * group : (b + 1) * group].astype(F32)[:, 32:40] for b in range(BATCH)]
    h_held[0] = jnp.concatenate(taps, axis=1).reshape(group * 16, LANES)
    turn_cos = turn_ref[0:rows, :]
    turn_sin = turn_ref[rows : 2 * rows, :]

    def forward(held, b, channels):
        pair = jnp.concatenate(
            [held[b, pl.ds(c, rows, stride=OWN), :].astype(BF16) for c in channels], axis=1
        )
        both = dot(first_ref[0 : 2 * rows, :], pair) + dot(first_ref[2 * rows : 4 * rows, :], pair)
        spectra = []
        for i in range(len(channels)):
            lanes = slice(i * LANES, (i + 1) * LANES)
            real, imag = both[0:rows, lanes], both[rows : 2 * rows, lanes]
            turned = jnp.concatenate(
                [real * turn_cos + imag * turn_sin, imag * turn_cos - real * turn_sin], axis=1
            )
            spectra.append(across(turned, forth_ref))
        return spectra

    def across(value, matrix_ref):
        high, low = split(value)
        width = 2 * LANES
        return (
            dot(high, matrix_ref[0:width, :])
            + dot(low, matrix_ref[0:width, :])
            + dot(high, matrix_ref[width : 2 * width, :])
        )

    def parts(spectrum):
        return spectrum[:, :LANES], spectrum[:, LANES:]

    def correlate(left, right):
        left_re, left_im = parts(left)
        right_re, right_im = parts(right)
        return jnp.concatenate(
            [left_re * right_re + left_im * right_im, left_im * right_re - left_re * right_im], axis=1
        )

    def backward(products):
        reals, imags = [], []
        for product in products:
            real, imag = parts(across(product, back_ref))
            reals.append(real * turn_cos - imag * turn_sin)
            imags.append(imag * turn_cos + real * turn_sin)
        stacked = jnp.concatenate([jnp.concatenate(reals, axis=1), jnp.concatenate(imags, axis=1)], axis=0)
        high, low = split(stacked)
        return dot(last_ref[0:rows, :], high) + dot(last_ref[0:rows, :], low) + dot(last_ref[rows : 2 * rows, :], high)

    for half in range(2):
        channels = (2 * half, 2 * half + 1)
        taps_spec = forward(h_held, 0, channels)
        grad_spec = [forward(g_held, b, channels) for b in range(BATCH)]
        for b in range(BATCH):
            result = backward([correlate(grad_spec[b][i], taps_spec[i]) for i in range(2)])
            for i in range(2):
                in_grad[b, pl.ds(channels[i], rows, stride=OWN), :] = result[:, i * LANES : (i + 1) * LANES]
        signal_spec = [forward(u_held, b, channels) for b in range(BATCH)]
        result = backward(
            [correlate(grad_spec[0][i], signal_spec[0][i]) + correlate(grad_spec[1][i], signal_spec[1][i]) for i in range(2)]
        )
        for i in range(2):
            taps_grad[half, pl.ds(i, rows, stride=2), :] = result[:, i * LANES : (i + 1) * LANES]
    for d in range(2):
        taps_out = taps_grad[d].reshape(group, 8, LANES)
        high = taps_out.astype(BF16).astype(F32)
        out_ref[d * group : (d + 1) * group] = jnp.concatenate(
            [in_grad[d].reshape(group, 16, LANES), high, taps_out - high], axis=1
        ).astype(BF16)


def shards(saved_input, output_grad, filter_taps):
    group = lax.axis_size("ctx")
    peers = 2 * group
    local_len, chan_count = filter_taps.shape
    seq = group * local_len
    rows = seq // LANES
    constants = [jnp.asarray(table) for table in tables(seq)]
    params = pltpu.CompilerParams(vmem_limit_bytes=48 * 1024 * 1024)
    own_taps = lax.dynamic_slice_in_dim(filter_taps, lax.axis_index("dp") * (local_len // 2), local_len // 2, 0)
    packed = pl.pallas_call(
        functools.partial(pack_kernel, peers, None),
        out_shape=jax.ShapeDtypeStruct((peers, 40, LANES), BF16),
        scratch_shapes=[pltpu.VMEM((peers * 40, LANES), F32)],
        compiler_params=params,
        name="pack",
    )(saved_input[0], output_grad[0], own_taps)
    received = lax.all_to_all(packed, ("dp", "ctx"), split_axis=0, concat_axis=0, tiled=True)
    results = pl.pallas_call(
        functools.partial(convolve_kernel, group),
        out_shape=jax.ShapeDtypeStruct((peers, 32, LANES), BF16),
        scratch_shapes=[
            pltpu.VMEM((BATCH, group * 16, LANES), F32),
            pltpu.VMEM((BATCH, group * 16, LANES), F32),
            pltpu.VMEM((1, group * 16, LANES), F32),
            pltpu.VMEM((BATCH, group * 16, LANES), F32),
            pltpu.VMEM((BATCH, group * 8, LANES), F32),
        ],
        compiler_params=params,
        name="convolve",
    )(received, *constants)
    returned = lax.all_to_all(results, ("dp", "ctx"), split_axis=0, concat_axis=0, tiled=True)
    input_grad, filter_grad = pl.pallas_call(
        functools.partial(unpack_kernel, peers),
        out_shape=(
            jax.ShapeDtypeStruct((local_len, chan_count), BF16),
            jax.ShapeDtypeStruct((local_len, chan_count // 2), F32),
        ),
        scratch_shapes=[pltpu.VMEM((peers * 32, LANES), F32)],
        compiler_params=params,
        name="unpack",
    )(returned)
    return input_grad[None], filter_grad


def solution(mesh):
    placed = (P("dp", "ctx", None), P("dp", "ctx", None), P("ctx", None))
    return jax.shard_map(
        shards,
        mesh=mesh,
        in_specs=placed,
        out_specs=(P("dp", "ctx", None), P("ctx", "dp")),
        check_vma=False,
    )
```

```python
import functools
import math

import jax
import jax.numpy as jnp
import ml_dtypes
import numpy as np
from jax import lax
from jax.experimental import pallas as pl
from jax.experimental.pallas import tpu as pltpu
from jax.sharding import PartitionSpec as P

LANES = 128
BF16 = jnp.bfloat16
F32 = jnp.float32
OWN = 4
BATCH = 2


def two_parts(matrix):
    high = matrix.astype(ml_dtypes.bfloat16)
    low = (matrix - high.astype(np.float64)).astype(ml_dtypes.bfloat16)
    return high, low


def turn(numerator, period):
    phase = (numerator % period) * (2.0 * math.pi / period)
    return np.cos(phase), np.sin(phase)


@functools.cache
def tables(seq):
    rows = seq // LANES
    k1 = np.arange(rows, dtype=np.int64)[:, None]
    a = np.arange(rows, dtype=np.int64)[None, :]
    r = np.arange(LANES, dtype=np.int64)
    cos_a, sin_a = turn((4 * k1 + 1) * a, 4 * rows)
    first = np.concatenate([cos_a, -sin_a], axis=0)
    last = np.concatenate([cos_a.T, -sin_a.T], axis=1) / seq
    cos_t, sin_t = turn((4 * k1 + 1) * r[None, :], 4 * seq)
    cos_r, sin_r = turn(r[:, None] * r[None, :], LANES)
    forth = np.block([[cos_r, -sin_r], [sin_r, cos_r]])
    back = np.block([[cos_r, sin_r], [-sin_r, cos_r]])
    return (
        np.concatenate(two_parts(first), axis=0),
        np.concatenate(two_parts(last), axis=0),
        np.concatenate(two_parts(forth), axis=0),
        np.concatenate(two_parts(back), axis=0),
        np.concatenate([cos_t, sin_t], axis=0).astype(np.float32),
    )


def dot(left, right):
    return jnp.dot(left, right, preferred_element_type=F32)


def split(value):
    high = value.astype(BF16)
    return high, (value - high.astype(F32)).astype(BF16)


def pack_kernel(peers, u_ref, g_ref, h_ref, out_ref, landed, taps_landed, held, sems):
    share = taps_landed.shape[0]
    own = pl.multiple_of(lax.axis_index("dp") * share, share)
    arrivals = (
        (pltpu.make_async_copy(u_ref, landed.at[0], sems.at[0]), landed.at[0], 0),
        (pltpu.make_async_copy(g_ref, landed.at[1], sems.at[1]), landed.at[1], 16),
        (pltpu.make_async_copy(h_ref.at[pl.ds(own, share), :], taps_landed, sems.at[2]), taps_landed, 32),
    )
    for copy, _, _ in arrivals:
        copy.start()
    for copy, block, first_row in arrivals:
        copy.wait()
        for q in range(block.shape[0] // LANES):
            flipped = block[q * LANES : (q + 1) * LANES, :].astype(F32).T
            for c in range(OWN):
                row = first_row + OWN * q + c
                held[pl.ds(row, peers, stride=40), :] = flipped[c * peers : (c + 1) * peers, :]
    out_ref[...] = held[...].reshape(peers, 40, LANES).astype(BF16)


def unpack_kernel(peers, in_ref, input_ref, filter_ref, held, input_block, filter_block, sems):
    blocks = input_ref.shape[0] // LANES
    held[...] = in_ref[...].astype(F32).reshape(peers * 32, LANES)
    leaving = []
    for q in range(blocks):
        rows = slice(q * LANES, (q + 1) * LANES)
        for c in range(OWN):
            piece = held[pl.ds(OWN * q + c, peers, stride=32), :]
            input_block[rows, c * peers : (c + 1) * peers] = piece.T.astype(BF16)
        leaving.append(pltpu.make_async_copy(input_block.at[rows], input_ref.at[rows], sems.at[2 * q]))
        leaving[-1].start()
        for c in range(OWN // 2):
            high = held[pl.ds(16 + 2 * q + c, peers, stride=32), :]
            low = held[pl.ds(24 + 2 * q + c, peers, stride=32), :]
            filter_block[rows, c * peers : (c + 1) * peers] = (high + low).T
        leaving.append(pltpu.make_async_copy(filter_block.at[rows], filter_ref.at[rows], sems.at[2 * q + 1]))
        leaving[-1].start()
    for copy in leaving:
        copy.wait()


def convolve_kernel(group, in_ref, first_ref, last_ref, forth_ref, back_ref, turn_ref, out_ref, u_held, g_held, h_held, in_grad, taps_grad):
    rows = group * OWN
    for b in range(BATCH):
        got = in_ref[b * group : (b + 1) * group].astype(F32)
        u_held[b] = got[:, 0:16].reshape(group * 16, LANES)
        g_held[b] = got[:, 16:32].reshape(group * 16, LANES)
    taps = [in_ref[b * group : (b + 1) * group].astype(F32)[:, 32:40] for b in range(BATCH)]
    h_held[0] = jnp.concatenate(taps, axis=1).reshape(group * 16, LANES)
    turn_cos = turn_ref[0:rows, :]
    turn_sin = turn_ref[rows : 2 * rows, :]

    def forward(held, b, channels):
        pair = jnp.concatenate(
            [held[b, pl.ds(c, rows, stride=OWN), :].astype(BF16) for c in channels], axis=1
        )
        both = dot(first_ref[0 : 2 * rows, :], pair) + dot(first_ref[2 * rows : 4 * rows, :], pair)
        spectra = []
        for i in range(len(channels)):
            lanes = slice(i * LANES, (i + 1) * LANES)
            real, imag = both[0:rows, lanes], both[rows : 2 * rows, lanes]
            turned = jnp.concatenate(
                [real * turn_cos + imag * turn_sin, imag * turn_cos - real * turn_sin], axis=1
            )
            spectra.append(across(turned, forth_ref))
        return spectra

    def across(value, matrix_ref):
        high, low = split(value)
        width = 2 * LANES
        return (
            dot(high, matrix_ref[0:width, :])
            + dot(low, matrix_ref[0:width, :])
            + dot(high, matrix_ref[width : 2 * width, :])
        )

    def parts(spectrum):
        return spectrum[:, :LANES], spectrum[:, LANES:]

    def correlate(left, right):
        left_re, left_im = parts(left)
        right_re, right_im = parts(right)
        return jnp.concatenate(
            [left_re * right_re + left_im * right_im, left_im * right_re - left_re * right_im], axis=1
        )

    def backward(products):
        reals, imags = [], []
        for product in products:
            real, imag = parts(across(product, back_ref))
            reals.append(real * turn_cos - imag * turn_sin)
            imags.append(imag * turn_cos + real * turn_sin)
        stacked = jnp.concatenate([jnp.concatenate(reals, axis=1), jnp.concatenate(imags, axis=1)], axis=0)
        high, low = split(stacked)
        return dot(last_ref[0:rows, :], high) + dot(last_ref[0:rows, :], low) + dot(last_ref[rows : 2 * rows, :], high)

    for half in range(2):
        channels = (2 * half, 2 * half + 1)
        taps_spec = forward(h_held, 0, channels)
        grad_spec = [forward(g_held, b, channels) for b in range(BATCH)]
        for b in range(BATCH):
            result = backward([correlate(grad_spec[b][i], taps_spec[i]) for i in range(2)])
            for i in range(2):
                in_grad[b, pl.ds(channels[i], rows, stride=OWN), :] = result[:, i * LANES : (i + 1) * LANES]
        signal_spec = [forward(u_held, b, channels) for b in range(BATCH)]
        result = backward(
            [correlate(grad_spec[0][i], signal_spec[0][i]) + correlate(grad_spec[1][i], signal_spec[1][i]) for i in range(2)]
        )
        for i in range(2):
            taps_grad[half, pl.ds(i, rows, stride=2), :] = result[:, i * LANES : (i + 1) * LANES]
    for d in range(2):
        taps_out = taps_grad[d].reshape(group, 8, LANES)
        high = taps_out.astype(BF16).astype(F32)
        out_ref[d * group : (d + 1) * group] = jnp.concatenate(
            [in_grad[d].reshape(group, 16, LANES), high, taps_out - high], axis=1
        ).astype(BF16)


def shards(saved_input, output_grad, filter_taps):
    group = lax.axis_size("ctx")
    peers = 2 * group
    local_len, chan_count = filter_taps.shape
    seq = group * local_len
    rows = seq // LANES
    constants = [jnp.asarray(table) for table in tables(seq)]
    params = pltpu.CompilerParams(vmem_limit_bytes=48 * 1024 * 1024)
    local = pl.BlockSpec(memory_space=pltpu.VMEM)
    far = pl.BlockSpec(memory_space=pltpu.HBM)
    packed = pl.pallas_call(
        functools.partial(pack_kernel, peers),
        out_shape=jax.ShapeDtypeStruct((peers, 40, LANES), BF16),
        in_specs=[far] * 3,
        out_specs=local,
        scratch_shapes=[
            pltpu.VMEM((2, local_len, chan_count), BF16),
            pltpu.VMEM((local_len // 2, chan_count), BF16),
            pltpu.VMEM((peers * 40, LANES), F32),
            pltpu.SemaphoreType.DMA((3,)),
        ],
        compiler_params=params,
        name="pack",
    )(*[pltpu.with_memory_space_constraint(x, pltpu.HBM) for x in (saved_input[0], output_grad[0], filter_taps)])
    received = lax.all_to_all(packed, ("dp", "ctx"), split_axis=0, concat_axis=0, tiled=True)
    results = pl.pallas_call(
        functools.partial(convolve_kernel, group),
        out_shape=jax.ShapeDtypeStruct((peers, 32, LANES), BF16),
        scratch_shapes=[
            pltpu.VMEM((BATCH, group * 16, LANES), F32),
            pltpu.VMEM((BATCH, group * 16, LANES), F32),
            pltpu.VMEM((1, group * 16, LANES), F32),
            pltpu.VMEM((BATCH, group * 16, LANES), F32),
            pltpu.VMEM((BATCH, group * 8, LANES), F32),
        ],
        compiler_params=params,
        name="convolve",
    )(received, *constants)
    returned = lax.all_to_all(results, ("dp", "ctx"), split_axis=0, concat_axis=0, tiled=True)
    input_grad, filter_grad = pl.pallas_call(
        functools.partial(unpack_kernel, peers),
        out_shape=(
            jax.ShapeDtypeStruct((local_len, chan_count), BF16),
            jax.ShapeDtypeStruct((local_len, chan_count // 2), F32),
        ),
        in_specs=[local],
        out_specs=(far, far),
        scratch_shapes=[
            pltpu.VMEM((peers * 32, LANES), F32),
            pltpu.VMEM((local_len, chan_count), BF16),
            pltpu.VMEM((local_len, chan_count // 2), F32),
            pltpu.SemaphoreType.DMA((2 * (local_len // LANES),)),
        ],
        compiler_params=params,
        name="unpack",
    )(returned)
    return input_grad[None], filter_grad


def solution(mesh):
    placed = (P("dp", "ctx", None), P("dp", "ctx", None), P("ctx", None))
    return jax.shard_map(
        shards,
        mesh=mesh,
        in_specs=placed,
        out_specs=(P("dp", "ctx", None), P("ctx", "dp")),
        check_vma=False,
    )
```

```python
import functools
import math

import jax
import jax.numpy as jnp
import ml_dtypes
import numpy as np
from jax import lax
from jax.experimental import pallas as pl
from jax.experimental.pallas import tpu as pltpu
from jax.sharding import PartitionSpec as P

LANES = 128
BF16 = jnp.bfloat16
F32 = jnp.float32
OWN = 4
BATCH = 2
STEPS = 959.0


def two_parts(matrix):
    high = matrix.astype(ml_dtypes.bfloat16)
    low = (matrix - high.astype(np.float64)).astype(ml_dtypes.bfloat16)
    return high, low


def turn(numerator, period):
    phase = (numerator % period) * (2.0 * math.pi / period)
    return np.cos(phase), np.sin(phase)


@functools.cache
def tables(seq):
    rows = seq // LANES
    k1 = np.arange(rows, dtype=np.int64)[:, None]
    a = np.arange(rows, dtype=np.int64)[None, :]
    r = np.arange(LANES, dtype=np.int64)
    cos_a, sin_a = turn((4 * k1 + 1) * a, 4 * rows)
    first = np.concatenate([cos_a, -sin_a], axis=0)
    last = np.concatenate([cos_a.T, -sin_a.T], axis=1) / seq
    cos_t, sin_t = turn((4 * k1 + 1) * r[None, :], 4 * seq)
    cos_r, sin_r = turn(r[:, None] * r[None, :], LANES)
    forth = np.block([[cos_r, -sin_r], [sin_r, cos_r]])
    back = np.block([[cos_r, sin_r], [-sin_r, cos_r]])
    return (
        np.concatenate(two_parts(first), axis=0),
        np.concatenate(two_parts(last), axis=0),
        np.concatenate(two_parts(forth), axis=0),
        np.concatenate(two_parts(back), axis=0),
        np.concatenate([cos_t, sin_t], axis=0).astype(np.float32),
    )


def dot(left, right):
    return jnp.dot(left, right, preferred_element_type=F32)


def split(value):
    high = value.astype(BF16)
    return high, (value - high.astype(F32)).astype(BF16)


def word(code, exponent):
    negative = code >= 128.0
    size = jnp.where(negative, code, code + 128.0) * (1 / 128) * jnp.exp2(exponent)
    return jnp.where(negative, -size, size)


def code_of(held_word):
    size = jnp.abs(held_word)
    exponent = jnp.floor(jnp.log2(size) + 0.002)
    digits = jnp.floor(size * jnp.exp2(7.0 - exponent) + 0.5)
    return jnp.where(held_word < 0.0, digits, digits - 128.0), exponent


def encode(one, two):
    top = jnp.maximum(jnp.maximum(jnp.abs(one), jnp.abs(two)), 2.0**-115)
    exponent = jnp.floor(jnp.log2(top))
    scale = jnp.exp2(-exponent)
    one_code = jnp.floor(one * scale * STEPS + (2 * STEPS + 0.5))
    two_code = jnp.floor(two * scale * STEPS + (2 * STEPS + 0.5))
    coarse = jnp.floor(one_code * (1 / 16))
    rest = two_code * 16.0 + (one_code - 16.0 * coarse)
    upper = jnp.floor(rest * (1 / 256))
    return word(coarse, exponent), word(rest - 256.0 * upper, upper - 120.0)


def decode(first_word, second_word):
    coarse, exponent = code_of(first_word)
    lower, upper = code_of(second_word)
    rest = (upper + 120.0) * 256.0 + lower
    two_code = jnp.floor(rest * (1 / 16))
    one_code = 16.0 * coarse + (rest - 16.0 * two_code)
    scale = jnp.exp2(exponent) * (1 / STEPS)
    return (one_code - 2 * STEPS) * scale, (two_code - 2 * STEPS) * scale


def pack_kernel(peers, u_ref, g_ref, h_ref, out_ref, landed, taps_landed, held, sems):
    share = taps_landed.shape[0]
    own = pl.multiple_of(lax.axis_index("dp") * share, share)
    arrivals = (
        (pltpu.make_async_copy(u_ref, landed.at[0], sems.at[0]), landed.at[0], 0),
        (pltpu.make_async_copy(g_ref, landed.at[1], sems.at[1]), landed.at[1], 16),
        (pltpu.make_async_copy(h_ref.at[pl.ds(own, share), :], taps_landed, sems.at[2]), taps_landed, 32),
    )
    for copy, _, _ in arrivals:
        copy.start()
    for copy, block, first_row in arrivals:
        copy.wait()
        for q in range(block.shape[0] // LANES):
            flipped = block[q * LANES : (q + 1) * LANES, :].astype(F32).T
            for c in range(OWN):
                row = first_row + OWN * q + c
                held[pl.ds(row, peers, stride=40), :] = flipped[c * peers : (c + 1) * peers, :]
    out_ref[...] = held[...].reshape(peers, 40, LANES).astype(BF16)


def unpack_kernel(peers, in_ref, input_ref, filter_ref, held, input_block, filter_block, sems):
    blocks = input_ref.shape[0] // LANES
    held[...] = in_ref[...].astype(F32).reshape(peers * 24, LANES)
    leaving = []
    for q in range(blocks):
        rows = slice(q * LANES, (q + 1) * LANES)
        for c in range(OWN):
            piece = held[pl.ds(OWN * q + c, peers, stride=24), :]
            input_block[rows, c * peers : (c + 1) * peers] = piece.T.astype(BF16)
        leaving.append(pltpu.make_async_copy(input_block.at[rows], input_ref.at[rows], sems.at[2 * q]))
        leaving[-1].start()
        words = [held[pl.ds(16 + 2 * q + c, peers, stride=24), :] for c in range(2)]
        for c, piece in enumerate(decode(*words)):
            filter_block[rows, c * peers : (c + 1) * peers] = piece.T
        leaving.append(pltpu.make_async_copy(filter_block.at[rows], filter_ref.at[rows], sems.at[2 * q + 1]))
        leaving[-1].start()
    for copy in leaving:
        copy.wait()


def convolve_kernel(group, in_ref, first_ref, last_ref, forth_ref, back_ref, turn_ref, out_ref, u_held, g_held, h_held, in_grad, taps_grad):
    rows = group * OWN
    for b in range(BATCH):
        got = in_ref[b * group : (b + 1) * group].astype(F32)
        u_held[b] = got[:, 0:16].reshape(group * 16, LANES)
        g_held[b] = got[:, 16:32].reshape(group * 16, LANES)
    taps = [in_ref[b * group : (b + 1) * group].astype(F32)[:, 32:40] for b in range(BATCH)]
    h_held[0] = jnp.concatenate(taps, axis=1).reshape(group * 16, LANES)
    turn_cos = turn_ref[0:rows, :]
    turn_sin = turn_ref[rows : 2 * rows, :]

    def forward(held, b, channels):
        pair = jnp.concatenate(
            [held[b, pl.ds(c, rows, stride=OWN), :].astype(BF16) for c in channels], axis=1
        )
        both = dot(first_ref[0 : 2 * rows, :], pair) + dot(first_ref[2 * rows : 4 * rows, :], pair)
        spectra = []
        for i in range(len(channels)):
            lanes = slice(i * LANES, (i + 1) * LANES)
            real, imag = both[0:rows, lanes], both[rows : 2 * rows, lanes]
            turned = jnp.concatenate(
                [real * turn_cos + imag * turn_sin, imag * turn_cos - real * turn_sin], axis=1
            )
            spectra.append(across(turned, forth_ref))
        return spectra

    def across(value, matrix_ref):
        high, low = split(value)
        width = 2 * LANES
        return (
            dot(high, matrix_ref[0:width, :])
            + dot(low, matrix_ref[0:width, :])
            + dot(high, matrix_ref[width : 2 * width, :])
        )

    def parts(spectrum):
        return spectrum[:, :LANES], spectrum[:, LANES:]

    def correlate(left, right):
        left_re, left_im = parts(left)
        right_re, right_im = parts(right)
        return jnp.concatenate(
            [left_re * right_re + left_im * right_im, left_im * right_re - left_re * right_im], axis=1
        )

    def backward(products):
        reals, imags = [], []
        for product in products:
            real, imag = parts(across(product, back_ref))
            reals.append(real * turn_cos - imag * turn_sin)
            imags.append(imag * turn_cos + real * turn_sin)
        stacked = jnp.concatenate([jnp.concatenate(reals, axis=1), jnp.concatenate(imags, axis=1)], axis=0)
        high, low = split(stacked)
        return dot(last_ref[0:rows, :], high) + dot(last_ref[0:rows, :], low) + dot(last_ref[rows : 2 * rows, :], high)

    for half in range(2):
        channels = (2 * half, 2 * half + 1)
        taps_spec = forward(h_held, 0, channels)
        grad_spec = [forward(g_held, b, channels) for b in range(BATCH)]
        for b in range(BATCH):
            result = backward([correlate(grad_spec[b][i], taps_spec[i]) for i in range(2)])
            for i in range(2):
                in_grad[b, pl.ds(channels[i], rows, stride=OWN), :] = result[:, i * LANES : (i + 1) * LANES]
        signal_spec = [forward(u_held, b, channels) for b in range(BATCH)]
        result = backward(
            [correlate(grad_spec[0][i], signal_spec[0][i]) + correlate(grad_spec[1][i], signal_spec[1][i]) for i in range(2)]
        )
        for i, coded in enumerate(encode(result[:, :LANES], result[:, LANES:])):
            taps_grad[half, pl.ds(i, rows, stride=2), :] = coded
    for d in range(2):
        out_ref[d * group : (d + 1) * group] = jnp.concatenate(
            [in_grad[d].reshape(group, 16, LANES), taps_grad[d].reshape(group, 8, LANES)], axis=1
        ).astype(BF16)


def shards(saved_input, output_grad, filter_taps):
    group = lax.axis_size("ctx")
    peers = 2 * group
    local_len, chan_count = filter_taps.shape
    seq = group * local_len
    rows = seq // LANES
    constants = [jnp.asarray(table) for table in tables(seq)]
    params = pltpu.CompilerParams(vmem_limit_bytes=48 * 1024 * 1024)
    local = pl.BlockSpec(memory_space=pltpu.VMEM)
    far = pl.BlockSpec(memory_space=pltpu.HBM)
    packed = pl.pallas_call(
        functools.partial(pack_kernel, peers),
        out_shape=jax.ShapeDtypeStruct((peers, 40, LANES), BF16),
        in_specs=[far] * 3,
        out_specs=local,
        scratch_shapes=[
            pltpu.VMEM((2, local_len, chan_count), BF16),
            pltpu.VMEM((local_len // 2, chan_count), BF16),
            pltpu.VMEM((peers * 40, LANES), F32),
            pltpu.SemaphoreType.DMA((3,)),
        ],
        compiler_params=params,
        name="pack",
    )(*[pltpu.with_memory_space_constraint(x, pltpu.HBM) for x in (saved_input[0], output_grad[0], filter_taps)])
    received = lax.all_to_all(packed, ("dp", "ctx"), split_axis=0, concat_axis=0, tiled=True)
    results = pl.pallas_call(
        functools.partial(convolve_kernel, group),
        out_shape=jax.ShapeDtypeStruct((peers, 24, LANES), BF16),
        scratch_shapes=[
            pltpu.VMEM((BATCH, group * 16, LANES), F32),
            pltpu.VMEM((BATCH, group * 16, LANES), F32),
            pltpu.VMEM((1, group * 16, LANES), F32),
            pltpu.VMEM((BATCH, group * 16, LANES), F32),
            pltpu.VMEM((BATCH, group * 8, LANES), F32),
        ],
        compiler_params=params,
        name="convolve",
    )(received, *constants)
    returned = lax.all_to_all(results, ("dp", "ctx"), split_axis=0, concat_axis=0, tiled=True)
    input_grad, filter_grad = pl.pallas_call(
        functools.partial(unpack_kernel, peers),
        out_shape=(
            jax.ShapeDtypeStruct((local_len, chan_count), BF16),
            jax.ShapeDtypeStruct((local_len, chan_count // 2), F32),
        ),
        in_specs=[local],
        out_specs=(far, far),
        scratch_shapes=[
            pltpu.VMEM((peers * 24, LANES), F32),
            pltpu.VMEM((local_len, chan_count), BF16),
            pltpu.VMEM((local_len, chan_count // 2), F32),
            pltpu.SemaphoreType.DMA((2 * (local_len // LANES),)),
        ],
        compiler_params=params,
        name="unpack",
    )(returned)
    return input_grad[None], filter_grad


def solution(mesh):
    placed = (P("dp", "ctx", None), P("dp", "ctx", None), P("ctx", None))
    return jax.shard_map(
        shards,
        mesh=mesh,
        in_specs=placed,
        out_specs=(P("dp", "ctx", None), P("ctx", "dp")),
        check_vma=False,
    )
```

```python
import functools
import math

import jax
import jax.numpy as jnp
import ml_dtypes
import numpy as np
from jax import lax
from jax.experimental import pallas as pl
from jax.experimental.pallas import tpu as pltpu
from jax.sharding import PartitionSpec as P

LANES = 128
BF16 = jnp.bfloat16
F32 = jnp.float32
OWN = 4
BATCH = 2
STEPS = 959.0


def two_parts(matrix):
    high = matrix.astype(ml_dtypes.bfloat16)
    low = (matrix - high.astype(np.float64)).astype(ml_dtypes.bfloat16)
    return high, low


def three_parts(matrix, axis):
    high, low = two_parts(matrix)
    return np.concatenate([high, high, low], axis=axis)


def turn(numerator, period):
    phase = (numerator % period) * (2.0 * math.pi / period)
    return np.cos(phase), np.sin(phase)


@functools.cache
def tables(seq):
    rows = seq // (2 * LANES)
    k1 = np.arange(rows, dtype=np.int64)[:, None]
    a = np.arange(rows, dtype=np.int64)[None, :]
    r = np.arange(LANES, dtype=np.int64)
    cos_a, sin_a = turn((4 * k1 + 1) * a, 4 * rows)
    first = np.concatenate([cos_a, -sin_a], axis=0)
    last = np.concatenate([cos_a.T, -sin_a.T], axis=1) / seq
    cos_t, sin_t = turn((4 * k1 + 1) * np.arange(2 * LANES, dtype=np.int64)[None, :], 4 * seq)
    cos_h, sin_h = turn(r, 2 * LANES)
    cos_r, sin_r = turn(r[:, None] * r[None, :], LANES)
    forth = np.block([[cos_r, -sin_r], [sin_r, cos_r]])
    back = np.block([[cos_r, sin_r], [-sin_r, cos_r]])
    halves = np.concatenate([np.tile(cos_h, (8, 1)), np.tile(sin_h, (8, 1))], axis=1)
    return (
        np.concatenate(two_parts(first), axis=1),
        three_parts(last, 1),
        three_parts(forth, 0),
        three_parts(back, 0),
        np.concatenate([cos_t, sin_t, halves], axis=0).astype(np.float32),
    )


def dot(left, right):
    return jnp.dot(left, right, preferred_element_type=F32)


def split(value):
    high = value.astype(BF16)
    return high, (value - high.astype(F32)).astype(BF16)


def stack(value, axis):
    high, low = split(value)
    return jnp.concatenate([high, low, high], axis=axis)


def interleave(tasks, at_once):
    waiting, active = list(tasks), []
    while waiting or active:
        while waiting and len(active) < at_once:
            active.append(waiting.pop(0))
        for task in list(active):
            if next(task, "over") == "over":
                active.remove(task)


def word(code, exponent):
    negative = code >= 128.0
    size = jnp.where(negative, code, code + 128.0) * (1 / 128) * jnp.exp2(exponent)
    return jnp.where(negative, -size, size)


def code_of(held_word):
    size = jnp.abs(held_word)
    exponent = jnp.floor(jnp.log2(size) + 0.002)
    digits = jnp.floor(size * jnp.exp2(7.0 - exponent) + 0.5)
    return jnp.where(held_word < 0.0, digits, digits - 128.0), exponent


def encode(one, two):
    top = jnp.maximum(jnp.maximum(jnp.abs(one), jnp.abs(two)), 2.0**-115)
    exponent = jnp.floor(jnp.log2(top))
    scale = jnp.exp2(-exponent)
    one_code = jnp.floor(one * scale * STEPS + (2 * STEPS + 0.5))
    two_code = jnp.floor(two * scale * STEPS + (2 * STEPS + 0.5))
    coarse = jnp.floor(one_code * (1 / 16))
    rest = two_code * 16.0 + (one_code - 16.0 * coarse)
    upper = jnp.floor(rest * (1 / 256))
    return word(coarse, exponent), word(rest - 256.0 * upper, upper - 120.0)


def decode(first_word, second_word):
    coarse, exponent = code_of(first_word)
    lower, upper = code_of(second_word)
    rest = (upper + 120.0) * 256.0 + lower
    two_code = jnp.floor(rest * (1 / 16))
    one_code = 16.0 * coarse + (rest - 16.0 * two_code)
    scale = jnp.exp2(exponent) * (1 / STEPS)
    return (one_code - 2 * STEPS) * scale, (two_code - 2 * STEPS) * scale


def pack_kernel(peers, u_ref, g_ref, h_ref, out_ref, landed, taps_landed, held, sems):
    share = taps_landed.shape[0]
    own = pl.multiple_of(lax.axis_index("dp") * share, share)
    arrivals = (
        (pltpu.make_async_copy(u_ref, landed.at[0], sems.at[0]), landed.at[0], 0),
        (pltpu.make_async_copy(g_ref, landed.at[1], sems.at[1]), landed.at[1], 16),
        (pltpu.make_async_copy(h_ref.at[pl.ds(own, share), :], taps_landed, sems.at[2]), taps_landed, 32),
    )
    for copy, _, _ in arrivals:
        copy.start()
    for copy, block, first_row in arrivals:
        copy.wait()
        for q in range(block.shape[0] // LANES):
            flipped = block[q * LANES : (q + 1) * LANES, :].astype(F32).T
            for c in range(OWN):
                row = first_row + OWN * q + c
                held[pl.ds(row, peers, stride=40), :] = flipped[c * peers : (c + 1) * peers, :]
    out_ref[...] = held[...].reshape(peers, 40, LANES).astype(BF16)


def unpack_kernel(peers, in_ref, input_ref, filter_ref, held, input_block, filter_block, sems):
    blocks = input_ref.shape[0] // LANES
    held[...] = in_ref[...].astype(F32).reshape(peers * 24, LANES)
    leaving = []
    for q in range(blocks):
        rows = slice(q * LANES, (q + 1) * LANES)
        for c in range(OWN):
            piece = held[pl.ds(OWN * q + c, peers, stride=24), :]
            input_block[rows, c * peers : (c + 1) * peers] = piece.T.astype(BF16)
        leaving.append(pltpu.make_async_copy(input_block.at[rows], input_ref.at[rows], sems.at[2 * q]))
        leaving[-1].start()
        words = [held[pl.ds(16 + 2 * q + c, peers, stride=24), :] for c in range(2)]
        for c, piece in enumerate(decode(*words)):
            filter_block[rows, c * peers : (c + 1) * peers] = piece.T
        leaving.append(pltpu.make_async_copy(filter_block.at[rows], filter_ref.at[rows], sems.at[2 * q + 1]))
        leaving[-1].start()
    for copy in leaving:
        copy.wait()


def convolve_kernel(group, in_ref, first_ref, last_ref, forth_ref, back_ref, turn_ref, out_ref, u_held, g_held, h_held, in_grad, taps_grad):
    rows = 2 * group
    for b in range(BATCH):
        got = in_ref[b * group : (b + 1) * group].astype(F32)
        u_held[b] = got[:, 0:16].reshape(group * 16, LANES)
        g_held[b] = got[:, 16:32].reshape(group * 16, LANES)
    taps = [in_ref[b * group : (b + 1) * group].astype(F32)[:, 32:40] for b in range(BATCH)]
    h_held[0] = jnp.concatenate(taps, axis=1).reshape(group * 16, LANES)

    def columns(value):
        return value[:, :LANES], value[:, LANES:]

    def turns():
        turn_cos = columns(turn_ref[0:rows, :])
        turn_sin = columns(turn_ref[rows : 2 * rows, :])
        half_cos, half_sin = columns(turn_ref[2 * rows : 2 * rows + 1, :])
        return turn_cos, turn_sin, half_cos, half_sin

    spectra, finished = {}, {}

    def forward(name, held, b, c):
        values = jnp.concatenate(
            [held[b, pl.ds(OWN * q + c, rows, stride=2 * OWN), :].astype(BF16) for q in range(2)], axis=1
        )
        both = dot(first_ref[...], jnp.concatenate([values, values], axis=0))
        yield
        turn_cos, turn_sin, half_cos, half_sin = turns()
        turned = []
        for q in range(2):
            real, imag = columns(both[0:rows])[q], columns(both[rows : 2 * rows])[q]
            turned.append((real * turn_cos[q] + imag * turn_sin[q], imag * turn_cos[q] - real * turn_sin[q]))
        sum_re, sum_im = turned[0][0] + turned[1][0], turned[0][1] + turned[1][1]
        off_re, off_im = turned[0][0] - turned[1][0], turned[0][1] - turned[1][1]
        even = jnp.concatenate([sum_re, sum_im], axis=1)
        odd = jnp.concatenate(
            [off_re * half_cos + off_im * half_sin, off_im * half_cos - off_re * half_sin], axis=1
        )
        spectra[name, c] = dot(stack(jnp.concatenate([even, odd], axis=0), 1), forth_ref[...])
        yield

    def correlate(left, right, c):
        left_re, left_im = columns(spectra[left, c])
        right_re, right_im = columns(spectra[right, c])
        return jnp.concatenate(
            [left_re * right_re + left_im * right_im, left_im * right_re - left_re * right_im], axis=1
        )

    def backward(pairs, c, store):
        while not all((name, c) in spectra for pair in pairs for name in pair):
            yield
        product = functools.reduce(jnp.add, [correlate(left, right, c) for left, right in pairs])
        spread = dot(stack(product, 1), back_ref[...])
        yield
        turn_cos, turn_sin, half_cos, half_sin = turns()
        even_re, even_im = columns(spread[0:rows])
        real, imag = columns(spread[rows : 2 * rows])
        odd_re, odd_im = real * half_cos - imag * half_sin, imag * half_cos + real * half_sin
        reals, imags = [], []
        for q, (real, imag) in enumerate(((even_re + odd_re, even_im + odd_im), (even_re - odd_re, even_im - odd_im))):
            reals.append(real * turn_cos[q] - imag * turn_sin[q])
            imags.append(imag * turn_cos[q] + real * turn_sin[q])
        turned = jnp.concatenate([jnp.concatenate(reals, axis=1), jnp.concatenate(imags, axis=1)], axis=0)
        result = dot(last_ref[...], stack(turned, 0))
        yield
        store(result, c)

    def store_input(b):
        def store(result, c):
            for q in range(2):
                in_grad[b, pl.ds(OWN * q + c, rows, stride=2 * OWN), :] = columns(result)[q]

        return store

    def store_taps(result, c):
        finished[c] = result
        half = c // 2
        if 2 * half in finished and 2 * half + 1 in finished:
            for i, coded in enumerate(encode(finished[2 * half], finished[2 * half + 1])):
                for q in range(2):
                    taps_grad[half, pl.ds(2 * q + i, rows, stride=4), :] = columns(coded)[q]

    tasks = []
    for half in range(2):
        channels = (2 * half, 2 * half + 1)
        for name, held, b in (("g0", g_held, 0), ("g1", g_held, 1), ("h", h_held, 0), ("u0", u_held, 0), ("u1", u_held, 1)):
            tasks += [forward(name, held, b, c) for c in channels]
        for b in range(BATCH):
            tasks += [backward([(f"g{b}", "h")], c, store_input(b)) for c in channels]
        tasks += [backward([("g0", "u0"), ("g1", "u1")], c, store_taps) for c in channels]
    interleave(tasks, 5)
    for d in range(2):
        out_ref[d * group : (d + 1) * group] = jnp.concatenate(
            [in_grad[d].reshape(group, 16, LANES), taps_grad[d].reshape(group, 8, LANES)], axis=1
        ).astype(BF16)


def shards(saved_input, output_grad, filter_taps):
    group = lax.axis_size("ctx")
    peers = 2 * group
    local_len, chan_count = filter_taps.shape
    seq = group * local_len
    constants = [jnp.asarray(table) for table in tables(seq)]
    params = pltpu.CompilerParams(vmem_limit_bytes=48 * 1024 * 1024)
    local = pl.BlockSpec(memory_space=pltpu.VMEM)
    far = pl.BlockSpec(memory_space=pltpu.HBM)
    packed = pl.pallas_call(
        functools.partial(pack_kernel, peers),
        out_shape=jax.ShapeDtypeStruct((peers, 40, LANES), BF16),
        in_specs=[far] * 3,
        out_specs=local,
        scratch_shapes=[
            pltpu.VMEM((2, local_len, chan_count), BF16),
            pltpu.VMEM((local_len // 2, chan_count), BF16),
            pltpu.VMEM((peers * 40, LANES), F32),
            pltpu.SemaphoreType.DMA((3,)),
        ],
        compiler_params=params,
        name="pack",
    )(*[pltpu.with_memory_space_constraint(x, pltpu.HBM) for x in (saved_input[0], output_grad[0], filter_taps)])
    received = lax.all_to_all(packed, ("dp", "ctx"), split_axis=0, concat_axis=0, tiled=True)
    results = pl.pallas_call(
        functools.partial(convolve_kernel, group),
        out_shape=jax.ShapeDtypeStruct((peers, 24, LANES), BF16),
        scratch_shapes=[
            pltpu.VMEM((BATCH, group * 16, LANES), F32),
            pltpu.VMEM((BATCH, group * 16, LANES), F32),
            pltpu.VMEM((1, group * 16, LANES), F32),
            pltpu.VMEM((BATCH, group * 16, LANES), F32),
            pltpu.VMEM((BATCH, group * 8, LANES), F32),
        ],
        compiler_params=params,
        name="convolve",
    )(received, *constants)
    returned = lax.all_to_all(results, ("dp", "ctx"), split_axis=0, concat_axis=0, tiled=True)
    input_grad, filter_grad = pl.pallas_call(
        functools.partial(unpack_kernel, peers),
        out_shape=(
            jax.ShapeDtypeStruct((local_len, chan_count), BF16),
            jax.ShapeDtypeStruct((local_len, chan_count // 2), F32),
        ),
        in_specs=[local],
        out_specs=(far, far),
        scratch_shapes=[
            pltpu.VMEM((peers * 24, LANES), F32),
            pltpu.VMEM((local_len, chan_count), BF16),
            pltpu.VMEM((local_len, chan_count // 2), F32),
            pltpu.SemaphoreType.DMA((2 * (local_len // LANES),)),
        ],
        compiler_params=params,
        name="unpack",
    )(returned)
    return input_grad[None], filter_grad


def solution(mesh):
    placed = (P("dp", "ctx", None), P("dp", "ctx", None), P("ctx", None))
    return jax.shard_map(
        shards,
        mesh=mesh,
        in_specs=placed,
        out_specs=(P("dp", "ctx", None), P("ctx", "dp")),
        check_vma=False,
    )
```

```python
import functools
import math

import jax
import jax.numpy as jnp
import ml_dtypes
import numpy as np
from jax import lax
from jax.experimental import pallas as pl
from jax.experimental.pallas import tpu as pltpu
from jax.sharding import PartitionSpec as P

LANES = 128
BF16 = jnp.bfloat16
F32 = jnp.float32
OWN = 4
BATCH = 2
STEPS = 959.0


def two_parts(matrix):
    high = matrix.astype(ml_dtypes.bfloat16)
    low = (matrix - high.astype(np.float64)).astype(ml_dtypes.bfloat16)
    return high, low


def three_parts(matrix, axis):
    high, low = two_parts(matrix)
    return np.concatenate([high, high, low], axis=axis)


def turn(numerator, period):
    phase = (numerator % period) * (2.0 * math.pi / period)
    return np.cos(phase), np.sin(phase)


@functools.cache
def tables(seq):
    rows = seq // (2 * LANES)
    k1 = np.arange(rows, dtype=np.int64)[:, None]
    a = np.arange(rows, dtype=np.int64)[None, :]
    r = np.arange(LANES, dtype=np.int64)
    first, last = [], []
    for q in range(2):
        cos_a, sin_a = turn((4 * k1 + 1) * (2 * a + q), 8 * rows)
        first.append(np.concatenate(two_parts(np.concatenate([cos_a, -sin_a], axis=0)), axis=1))
        last.append(three_parts(np.concatenate([cos_a.T, -sin_a.T], axis=1) / seq, 1))
    turns = [np.concatenate(turn((4 * (k1 + m * rows) + 1) * r[None, :], 4 * seq), axis=1) for m in range(2)]
    cos_r, sin_r = turn(r[:, None] * r[None, :], LANES)
    forth = np.block([[cos_r, -sin_r], [sin_r, cos_r]])
    back = np.block([[cos_r, sin_r], [-sin_r, cos_r]])
    return (
        np.concatenate(first, axis=0),
        np.concatenate(last, axis=0),
        three_parts(forth, 0),
        three_parts(back, 0),
        np.concatenate(turns, axis=0).astype(np.float32),
    )


def dot(left, right):
    return jnp.dot(left, right, preferred_element_type=F32)


def split(value):
    high = value.astype(BF16)
    return high, (value - high.astype(F32)).astype(BF16)


def stack(value, axis):
    high, low = split(value)
    return jnp.concatenate([high, low, high], axis=axis)


def interleave(tasks, at_once):
    waiting, active = list(tasks), []
    while waiting or active:
        while waiting and len(active) < at_once:
            active.append(waiting.pop(0))
        for task in list(active):
            if next(task, "over") == "over":
                active.remove(task)


def word(code, exponent):
    negative = code >= 128.0
    size = jnp.where(negative, code, code + 128.0) * (1 / 128) * jnp.exp2(exponent)
    return jnp.where(negative, -size, size)


def code_of(held_word):
    size = jnp.abs(held_word)
    exponent = jnp.floor(jnp.log2(size) + 0.002)
    digits = jnp.floor(size * jnp.exp2(7.0 - exponent) + 0.5)
    return jnp.where(held_word < 0.0, digits, digits - 128.0), exponent


def encode(one, two):
    top = jnp.maximum(jnp.maximum(jnp.abs(one), jnp.abs(two)), 2.0**-115)
    exponent = jnp.floor(jnp.log2(top))
    scale = jnp.exp2(-exponent)
    one_code = jnp.floor(one * scale * STEPS + (2 * STEPS + 0.5))
    two_code = jnp.floor(two * scale * STEPS + (2 * STEPS + 0.5))
    coarse = jnp.floor(one_code * (1 / 16))
    rest = two_code * 16.0 + (one_code - 16.0 * coarse)
    upper = jnp.floor(rest * (1 / 256))
    return word(coarse, exponent), word(rest - 256.0 * upper, upper - 120.0)


def decode(first_word, second_word):
    coarse, exponent = code_of(first_word)
    lower, upper = code_of(second_word)
    rest = (upper + 120.0) * 256.0 + lower
    two_code = jnp.floor(rest * (1 / 16))
    one_code = 16.0 * coarse + (rest - 16.0 * two_code)
    scale = jnp.exp2(exponent) * (1 / STEPS)
    return (one_code - 2 * STEPS) * scale, (two_code - 2 * STEPS) * scale


def pack_kernel(peers, u_ref, g_ref, h_ref, out_ref, landed, taps_landed, held, sems):
    share = taps_landed.shape[0]
    own = pl.multiple_of(lax.axis_index("dp") * share, share)
    arrivals = (
        (pltpu.make_async_copy(u_ref, landed.at[0], sems.at[0]), landed.at[0], 0),
        (pltpu.make_async_copy(g_ref, landed.at[1], sems.at[1]), landed.at[1], 16),
        (pltpu.make_async_copy(h_ref.at[pl.ds(own, share), :], taps_landed, sems.at[2]), taps_landed, 32),
    )
    for copy, _, _ in arrivals:
        copy.start()
    for copy, block, first_row in arrivals:
        copy.wait()
        for q in range(block.shape[0] // LANES):
            flipped = block[q * LANES : (q + 1) * LANES, :].astype(F32).T
            for c in range(OWN):
                row = first_row + OWN * q + c
                held[pl.ds(row, peers, stride=40), :] = flipped[c * peers : (c + 1) * peers, :]
    out_ref[...] = held[...].reshape(peers, 40, LANES).astype(BF16)


def unpack_kernel(peers, in_ref, input_ref, filter_ref, held, input_block, filter_block, sems):
    blocks = input_ref.shape[0] // LANES
    held[...] = in_ref[...].astype(F32).reshape(peers * 24, LANES)
    leaving = []
    for q in range(blocks):
        rows = slice(q * LANES, (q + 1) * LANES)
        for c in range(OWN):
            piece = held[pl.ds(OWN * q + c, peers, stride=24), :]
            input_block[rows, c * peers : (c + 1) * peers] = piece.T.astype(BF16)
        leaving.append(pltpu.make_async_copy(input_block.at[rows], input_ref.at[rows], sems.at[2 * q]))
        leaving[-1].start()
        words = [held[pl.ds(16 + 2 * q + c, peers, stride=24), :] for c in range(2)]
        for c, piece in enumerate(decode(*words)):
            filter_block[rows, c * peers : (c + 1) * peers] = piece.T
        leaving.append(pltpu.make_async_copy(filter_block.at[rows], filter_ref.at[rows], sems.at[2 * q + 1]))
        leaving[-1].start()
    for copy in leaving:
        copy.wait()


def convolve_kernel(group, in_ref, first_ref, last_ref, forth_ref, back_ref, turn_ref, out_ref, u_held, g_held, h_held, in_grad, taps_grad):
    rows = 2 * group
    for b in range(BATCH):
        got = in_ref[b * group : (b + 1) * group].astype(F32)
        u_held[b] = got[:, 0:16].reshape(group * 16, LANES)
        g_held[b] = got[:, 16:32].reshape(group * 16, LANES)
    taps = [in_ref[b * group : (b + 1) * group].astype(F32)[:, 32:40] for b in range(BATCH)]
    h_held[0] = jnp.concatenate(taps, axis=1).reshape(group * 16, LANES)

    def columns(value):
        return value[:, :LANES], value[:, LANES:]

    def turns(m):
        return columns(turn_ref[m * rows : (m + 1) * rows, :])

    spectra = {}

    def forward(name, held, b, channels):
        both = []
        for q in range(2):
            values = jnp.concatenate(
                [held[b, pl.ds(OWN * q + c, rows, stride=2 * OWN), :].astype(BF16) for c in channels], axis=1
            )
            both.append(dot(first_ref[2 * rows * q : 2 * rows * (q + 1), :], jnp.concatenate([values, values], axis=0)))
        yield
        sums = (both[0] + both[1], both[0] - both[1])
        for i, c in enumerate(channels):
            turned = []
            for m in range(2):
                turn_cos, turn_sin = turns(m)
                real, imag = columns(sums[m][0:rows])[i], columns(sums[m][rows : 2 * rows])[i]
                turned.append(jnp.concatenate([real * turn_cos + imag * turn_sin, imag * turn_cos - real * turn_sin], axis=1))
            spectra[name, c] = dot(stack(jnp.concatenate(turned, axis=0), 1), forth_ref[...])
            yield
        yield

    def correlate(left, right, c):
        left_re, left_im = columns(spectra[left, c])
        right_re, right_im = columns(spectra[right, c])
        return jnp.concatenate(
            [left_re * right_re + left_im * right_im, left_im * right_re - left_re * right_im], axis=1
        )

    def backward(pairs, channels, store):
        while not all((name, c) in spectra for pair in pairs for name in pair for c in channels):
            yield
        spread = []
        for c in channels:
            product = functools.reduce(jnp.add, [correlate(left, right, c) for left, right in pairs])
            spread.append(dot(stack(product, 1), back_ref[...]))
            yield
        yield
        terms = []
        for one in spread:
            for m in range(2):
                turn_cos, turn_sin = turns(m)
                real, imag = columns(one[m * rows : (m + 1) * rows])
                terms.append(jnp.concatenate([real * turn_cos - imag * turn_sin, imag * turn_cos + real * turn_sin], axis=0))
        results = []
        for q in range(2):
            turned = jnp.concatenate([terms[2 * i] + terms[2 * i + 1] if q == 0 else terms[2 * i] - terms[2 * i + 1] for i in range(2)], axis=1)
            results.append(dot(last_ref[rows * q : rows * (q + 1), :], stack(turned, 0)))
            yield
        yield
        store(results, channels)

    def store_input(b):
        def store(results, channels):
            for q in range(2):
                for i, c in enumerate(channels):
                    in_grad[b, pl.ds(OWN * q + c, rows, stride=2 * OWN), :] = columns(results[q])[i]

        return store

    def store_taps(results, channels):
        for q in range(2):
            for i, coded in enumerate(encode(*columns(results[q]))):
                taps_grad[channels[0] // 2, pl.ds(2 * q + i, rows, stride=4), :] = coded

    def forwards(names, half):
        held = {"g0": (g_held, 0), "g1": (g_held, 1), "h": (h_held, 0), "u0": (u_held, 0), "u1": (u_held, 1)}
        return [forward(name, *held[name], (2 * half, 2 * half + 1)) for name in names]

    def inputs(half):
        return [backward([(f"g{b}", "h")], (2 * half, 2 * half + 1), store_input(b)) for b in range(BATCH)]

    def taps_of(half):
        return [backward([("g0", "u0"), ("g1", "u1")], (2 * half, 2 * half + 1), store_taps)]

    later, ready = forwards(("u0", "u1", "g0", "g1", "h"), 1), inputs(0) + taps_of(0)
    tasks = forwards(("g0", "g1", "h", "u0", "u1"), 0)
    tasks += [later[0], ready[0], later[1], ready[1], later[2], later[3], ready[2], later[4]]
    tasks += taps_of(1) + inputs(1)
    interleave(tasks, 6)
    for d in range(2):
        out_ref[d * group : (d + 1) * group] = jnp.concatenate(
            [in_grad[d].reshape(group, 16, LANES), taps_grad[d].reshape(group, 8, LANES)], axis=1
        ).astype(BF16)


def shards(saved_input, output_grad, filter_taps):
    group = lax.axis_size("ctx")
    peers = 2 * group
    local_len, chan_count = filter_taps.shape
    seq = group * local_len
    constants = [jnp.asarray(table) for table in tables(seq)]
    params = pltpu.CompilerParams(vmem_limit_bytes=48 * 1024 * 1024)
    local = pl.BlockSpec(memory_space=pltpu.VMEM)
    far = pl.BlockSpec(memory_space=pltpu.HBM)
    packed = pl.pallas_call(
        functools.partial(pack_kernel, peers),
        out_shape=jax.ShapeDtypeStruct((peers, 40, LANES), BF16),
        in_specs=[far] * 3,
        out_specs=local,
        scratch_shapes=[
            pltpu.VMEM((2, local_len, chan_count), BF16),
            pltpu.VMEM((local_len // 2, chan_count), BF16),
            pltpu.VMEM((peers * 40, LANES), F32),
            pltpu.SemaphoreType.DMA((3,)),
        ],
        compiler_params=params,
        name="pack",
    )(*[pltpu.with_memory_space_constraint(x, pltpu.HBM) for x in (saved_input[0], output_grad[0], filter_taps)])
    received = lax.all_to_all(packed, ("dp", "ctx"), split_axis=0, concat_axis=0, tiled=True)
    results = pl.pallas_call(
        functools.partial(convolve_kernel, group),
        out_shape=jax.ShapeDtypeStruct((peers, 24, LANES), BF16),
        scratch_shapes=[
            pltpu.VMEM((BATCH, group * 16, LANES), F32),
            pltpu.VMEM((BATCH, group * 16, LANES), F32),
            pltpu.VMEM((1, group * 16, LANES), F32),
            pltpu.VMEM((BATCH, group * 16, LANES), F32),
            pltpu.VMEM((BATCH, group * 8, LANES), F32),
        ],
        compiler_params=params,
        name="convolve",
    )(received, *constants)
    returned = lax.all_to_all(results, ("dp", "ctx"), split_axis=0, concat_axis=0, tiled=True)
    input_grad, filter_grad = pl.pallas_call(
        functools.partial(unpack_kernel, peers),
        out_shape=(
            jax.ShapeDtypeStruct((local_len, chan_count), BF16),
            jax.ShapeDtypeStruct((local_len, chan_count // 2), F32),
        ),
        in_specs=[local],
        out_specs=(far, far),
        scratch_shapes=[
            pltpu.VMEM((peers * 24, LANES), F32),
            pltpu.VMEM((local_len, chan_count), BF16),
            pltpu.VMEM((local_len, chan_count // 2), F32),
            pltpu.SemaphoreType.DMA((2 * (local_len // LANES),)),
        ],
        compiler_params=params,
        name="unpack",
    )(returned)
    return input_grad[None], filter_grad


def solution(mesh):
    placed = (P("dp", "ctx", None), P("dp", "ctx", None), P("ctx", None))
    return jax.shard_map(
        shards,
        mesh=mesh,
        in_specs=placed,
        out_specs=(P("dp", "ctx", None), P("ctx", "dp")),
        check_vma=False,
    )
```

```python
import functools
import math

import jax
import jax.numpy as jnp
import ml_dtypes
import numpy as np
from jax import lax
from jax.experimental import pallas as pl
from jax.experimental.pallas import tpu as pltpu
from jax.sharding import PartitionSpec as P

LANES = 128
BF16 = jnp.bfloat16
F32 = jnp.float32
OWN = 4
BATCH = 2
STEPS = 959.0


def two_parts(matrix):
    high = matrix.astype(ml_dtypes.bfloat16)
    low = (matrix - high.astype(np.float64)).astype(ml_dtypes.bfloat16)
    return high, low


def three_parts(matrix, axis):
    high, low = two_parts(matrix)
    return np.concatenate([high, high, low], axis=axis)


def turn(numerator, period):
    phase = (numerator % period) * (2.0 * math.pi / period)
    return np.cos(phase), np.sin(phase)


@functools.cache
def tables(seq):
    rows = seq // (2 * LANES)
    k1 = np.arange(rows, dtype=np.int64)[:, None]
    a = np.arange(rows, dtype=np.int64)[None, :]
    r = np.arange(LANES, dtype=np.int64)
    first, last = [], []
    for q in range(2):
        cos_a, sin_a = turn((4 * k1 + 1) * (2 * a + q), 8 * rows)
        first.append(np.concatenate(two_parts(np.concatenate([cos_a, -sin_a], axis=0)), axis=1))
        last.append(three_parts(np.concatenate([cos_a.T, -sin_a.T], axis=1) / seq, 1))
    turns = [np.concatenate(turn((4 * (k1 + m * rows) + 1) * r[None, :], 4 * seq), axis=1) for m in range(2)]
    cos_r, sin_r = turn(r[:, None] * r[None, :], LANES)
    forth = np.block([[cos_r, -sin_r], [sin_r, cos_r]])
    back = np.block([[cos_r, sin_r], [-sin_r, cos_r]])
    return (
        np.concatenate(first, axis=0),
        np.concatenate(last, axis=0),
        three_parts(forth, 0),
        three_parts(back, 0),
        np.concatenate(turns, axis=0).astype(np.float32),
    )


def dot(left, right):
    return jnp.dot(left, right, preferred_element_type=F32)


def split(value):
    high = value.astype(BF16)
    return high, (value - high.astype(F32)).astype(BF16)


def stack(value, axis):
    high, low = split(value)
    return jnp.concatenate([high, low, high], axis=axis)


def interleave(tasks, at_once):
    waiting, active = list(tasks), []
    while waiting or active:
        while waiting and len(active) < at_once:
            active.append(waiting.pop(0))
        for task in list(active):
            if next(task, "over") == "over":
                active.remove(task)


def word(code, exponent):
    negative = code >= 128.0
    size = jnp.where(negative, code, code + 128.0) * (1 / 128) * jnp.exp2(exponent)
    return jnp.where(negative, -size, size)


def code_of(held_word):
    size = jnp.abs(held_word)
    exponent = jnp.floor(jnp.log2(size) + 0.002)
    digits = jnp.floor(size * jnp.exp2(7.0 - exponent) + 0.5)
    return jnp.where(held_word < 0.0, digits, digits - 128.0), exponent


def encode(one, two):
    top = jnp.maximum(jnp.maximum(jnp.abs(one), jnp.abs(two)), 2.0**-115)
    exponent = jnp.floor(jnp.log2(top))
    scale = jnp.exp2(-exponent)
    one_code = jnp.floor(one * scale * STEPS + (2 * STEPS + 0.5))
    two_code = jnp.floor(two * scale * STEPS + (2 * STEPS + 0.5))
    coarse = jnp.floor(one_code * (1 / 16))
    rest = two_code * 16.0 + (one_code - 16.0 * coarse)
    upper = jnp.floor(rest * (1 / 256))
    return word(coarse, exponent), word(rest - 256.0 * upper, upper - 120.0)


def decode(first_word, second_word):
    coarse, exponent = code_of(first_word)
    lower, upper = code_of(second_word)
    rest = (upper + 120.0) * 256.0 + lower
    two_code = jnp.floor(rest * (1 / 16))
    one_code = 16.0 * coarse + (rest - 16.0 * two_code)
    scale = jnp.exp2(exponent) * (1 / STEPS)
    return (one_code - 2 * STEPS) * scale, (two_code - 2 * STEPS) * scale


def pack_kernel(peers, u_ref, g_ref, h_ref, out_ref, landed, taps_landed, held, sems):
    share = taps_landed.shape[0]
    own = pl.multiple_of(lax.axis_index("dp") * share, share)
    arrivals = (
        (pltpu.make_async_copy(h_ref.at[pl.ds(own, share), :], taps_landed, sems.at[2]), taps_landed, 32),
        (pltpu.make_async_copy(u_ref, landed.at[0], sems.at[0]), landed.at[0], 0),
        (pltpu.make_async_copy(g_ref, landed.at[1], sems.at[1]), landed.at[1], 16),
    )
    for copy, _, _ in arrivals:
        copy.start()
    for copy, block, first_row in arrivals:
        copy.wait()
        for q in range(block.shape[0] // LANES):
            flipped = block[q * LANES : (q + 1) * LANES, :].astype(F32).T
            for c in range(OWN):
                row = first_row + OWN * q + c
                held[pl.ds(row, peers, stride=40), :] = flipped[c * peers : (c + 1) * peers, :]
    out_ref[...] = held[...].reshape(peers, 40, LANES).astype(BF16)


def unpack_kernel(peers, in_ref, input_ref, filter_ref, held, input_block, filter_block, sems):
    blocks = input_ref.shape[0] // LANES
    held[...] = in_ref[...].astype(F32).reshape(peers * 24, LANES)
    leaving = []
    for q in range(blocks):
        rows = slice(q * LANES, (q + 1) * LANES)
        words = [held[pl.ds(16 + 2 * q + c, peers, stride=24), :] for c in range(2)]
        for c, piece in enumerate(decode(*words)):
            filter_block[rows, c * peers : (c + 1) * peers] = piece.T
        leaving.append(pltpu.make_async_copy(filter_block.at[rows], filter_ref.at[rows], sems.at[q]))
        leaving[-1].start()
    for q in range(blocks):
        rows = slice(q * LANES, (q + 1) * LANES)
        for c in range(OWN):
            piece = held[pl.ds(OWN * q + c, peers, stride=24), :]
            input_block[rows, c * peers : (c + 1) * peers] = piece.T.astype(BF16)
        leaving.append(pltpu.make_async_copy(input_block.at[rows], input_ref.at[rows], sems.at[blocks + q]))
        leaving[-1].start()
    for copy in leaving:
        copy.wait()


def convolve_kernel(group, in_ref, first_ref, last_ref, forth_ref, back_ref, turn_ref, out_ref, u_held, g_held, h_held, in_grad, taps_grad):
    rows = 2 * group
    for b in range(BATCH):
        got = in_ref[b * group : (b + 1) * group].astype(F32)
        u_held[b] = got[:, 0:16].reshape(group * 16, LANES)
        g_held[b] = got[:, 16:32].reshape(group * 16, LANES)
    taps = [in_ref[b * group : (b + 1) * group].astype(F32)[:, 32:40] for b in range(BATCH)]
    h_held[0] = jnp.concatenate(taps, axis=1).reshape(group * 16, LANES)

    def columns(value):
        return value[:, :LANES], value[:, LANES:]

    def turns(m):
        return columns(turn_ref[m * rows : (m + 1) * rows, :])

    spectra = {}

    def forward(name, held, b, channels):
        both = []
        for q in range(2):
            values = jnp.concatenate(
                [held[b, pl.ds(OWN * q + c, rows, stride=2 * OWN), :].astype(BF16) for c in channels], axis=1
            )
            both.append(dot(first_ref[2 * rows * q : 2 * rows * (q + 1), :], jnp.concatenate([values, values], axis=0)))
        yield
        sums = (both[0] + both[1], both[0] - both[1])
        turned = []
        for i, c in enumerate(channels):
            for m in range(2):
                turn_cos, turn_sin = turns(m)
                real, imag = columns(sums[m][0:rows])[i], columns(sums[m][rows : 2 * rows])[i]
                turned.append(jnp.concatenate([real * turn_cos + imag * turn_sin, imag * turn_cos - real * turn_sin], axis=1))
        done = dot(stack(jnp.concatenate(turned, axis=0), 1), forth_ref[...])
        for i, c in enumerate(channels):
            spectra[name, c] = done[2 * rows * i : 2 * rows * (i + 1)]
        yield

    def correlate(left, right, c):
        left_re, left_im = columns(spectra[left, c])
        right_re, right_im = columns(spectra[right, c])
        return jnp.concatenate(
            [left_re * right_re + left_im * right_im, left_im * right_re - left_re * right_im], axis=1
        )

    def backward(pairs, channels, store):
        while not all((name, c) in spectra for pair in pairs for name in pair for c in channels):
            yield
        spread = []
        for c in channels:
            product = functools.reduce(jnp.add, [correlate(left, right, c) for left, right in pairs])
            spread.append(dot(stack(product, 1), back_ref[...]))
            yield
        yield
        terms = []
        for one in spread:
            for m in range(2):
                turn_cos, turn_sin = turns(m)
                real, imag = columns(one[m * rows : (m + 1) * rows])
                terms.append(jnp.concatenate([real * turn_cos - imag * turn_sin, imag * turn_cos + real * turn_sin], axis=0))
        results = []
        for q in range(2):
            turned = jnp.concatenate([terms[2 * i] + terms[2 * i + 1] if q == 0 else terms[2 * i] - terms[2 * i + 1] for i in range(2)], axis=1)
            results.append(dot(last_ref[rows * q : rows * (q + 1), :], stack(turned, 0)))
            yield
        yield
        store(results, channels)

    def store_input(b):
        def store(results, channels):
            for q in range(2):
                for i, c in enumerate(channels):
                    in_grad[b, pl.ds(OWN * q + c, rows, stride=2 * OWN), :] = columns(results[q])[i]

        return store

    def store_taps(results, channels):
        for q in range(2):
            for i, coded in enumerate(encode(*columns(results[q]))):
                taps_grad[channels[0] // 2, pl.ds(2 * q + i, rows, stride=4), :] = coded

    def forwards(names, half):
        held = {"g0": (g_held, 0), "g1": (g_held, 1), "h": (h_held, 0), "u0": (u_held, 0), "u1": (u_held, 1)}
        return [forward(name, *held[name], (2 * half, 2 * half + 1)) for name in names]

    def inputs(half):
        return [backward([(f"g{b}", "h")], (2 * half, 2 * half + 1), store_input(b)) for b in range(BATCH)]

    def taps_of(half):
        return [backward([("g0", "u0"), ("g1", "u1")], (2 * half, 2 * half + 1), store_taps)]

    later, ready = forwards(("u0", "u1", "g0", "g1", "h"), 1), inputs(0) + taps_of(0)
    tasks = forwards(("g0", "g1", "h", "u0", "u1"), 0)
    tasks += [later[0], ready[0], later[1], ready[1], later[2], later[3], ready[2], later[4]]
    tasks += taps_of(1) + inputs(1)
    interleave(tasks, 5)
    for d in range(2):
        out_ref[d * group : (d + 1) * group] = jnp.concatenate(
            [in_grad[d].reshape(group, 16, LANES), taps_grad[d].reshape(group, 8, LANES)], axis=1
        ).astype(BF16)


def shards(saved_input, output_grad, filter_taps):
    group = lax.axis_size("ctx")
    peers = 2 * group
    local_len, chan_count = filter_taps.shape
    seq = group * local_len
    constants = [jnp.asarray(table) for table in tables(seq)]
    params = pltpu.CompilerParams(vmem_limit_bytes=48 * 1024 * 1024)
    local = pl.BlockSpec(memory_space=pltpu.VMEM)
    far = pl.BlockSpec(memory_space=pltpu.HBM)
    packed = pl.pallas_call(
        functools.partial(pack_kernel, peers),
        out_shape=jax.ShapeDtypeStruct((peers, 40, LANES), BF16),
        in_specs=[far] * 3,
        out_specs=local,
        scratch_shapes=[
            pltpu.VMEM((2, local_len, chan_count), BF16),
            pltpu.VMEM((local_len // 2, chan_count), BF16),
            pltpu.VMEM((peers * 40, LANES), F32),
            pltpu.SemaphoreType.DMA((3,)),
        ],
        compiler_params=params,
        name="pack",
    )(*[pltpu.with_memory_space_constraint(x, pltpu.HBM) for x in (saved_input[0], output_grad[0], filter_taps)])
    received = lax.all_to_all(packed, ("dp", "ctx"), split_axis=0, concat_axis=0, tiled=True)
    results = pl.pallas_call(
        functools.partial(convolve_kernel, group),
        out_shape=jax.ShapeDtypeStruct((peers, 24, LANES), BF16),
        scratch_shapes=[
            pltpu.VMEM((BATCH, group * 16, LANES), F32),
            pltpu.VMEM((BATCH, group * 16, LANES), F32),
            pltpu.VMEM((1, group * 16, LANES), F32),
            pltpu.VMEM((BATCH, group * 16, LANES), F32),
            pltpu.VMEM((BATCH, group * 8, LANES), F32),
        ],
        compiler_params=params,
        name="convolve",
    )(received, *constants)
    returned = lax.all_to_all(results, ("dp", "ctx"), split_axis=0, concat_axis=0, tiled=True)
    input_grad, filter_grad = pl.pallas_call(
        functools.partial(unpack_kernel, peers),
        out_shape=(
            jax.ShapeDtypeStruct((local_len, chan_count), BF16),
            jax.ShapeDtypeStruct((local_len, chan_count // 2), F32),
        ),
        in_specs=[local],
        out_specs=(far, far),
        scratch_shapes=[
            pltpu.VMEM((peers * 24, LANES), F32),
            pltpu.VMEM((local_len, chan_count), BF16),
            pltpu.VMEM((local_len, chan_count // 2), F32),
            pltpu.SemaphoreType.DMA((2 * (local_len // LANES),)),
        ],
        compiler_params=params,
        name="unpack",
    )(returned)
    return input_grad[None], filter_grad


def solution(mesh):
    placed = (P("dp", "ctx", None), P("dp", "ctx", None), P("ctx", None))
    return jax.shard_map(
        shards,
        mesh=mesh,
        in_specs=placed,
        out_specs=(P("dp", "ctx", None), P("ctx", "dp")),
        check_vma=False,
    )
```

```python
import functools
import math

import jax
import jax.numpy as jnp
import ml_dtypes
import numpy as np
from jax import lax
from jax.experimental import pallas as pl
from jax.experimental.pallas import tpu as pltpu
from jax.sharding import PartitionSpec as P

LANES = 128
BF16 = jnp.bfloat16
F32 = jnp.float32
OWN = 4
BATCH = 2
STEPS = 959.0


def two_parts(matrix):
    high = matrix.astype(ml_dtypes.bfloat16)
    low = (matrix - high.astype(np.float64)).astype(ml_dtypes.bfloat16)
    return high, low


def three_parts(matrix, axis):
    high, low = two_parts(matrix)
    return np.concatenate([high, high, low], axis=axis)


def turn(numerator, period):
    phase = (numerator % period) * (2.0 * math.pi / period)
    return np.cos(phase), np.sin(phase)


@functools.cache
def tables(seq):
    rows = seq // (2 * LANES)
    k1 = np.arange(rows, dtype=np.int64)[:, None]
    a = np.arange(rows, dtype=np.int64)[None, :]
    r = np.arange(LANES, dtype=np.int64)
    first, last = [], []
    for q in range(2):
        cos_a, sin_a = turn((4 * k1 + 1) * (2 * a + q), 8 * rows)
        first.append(np.concatenate(two_parts(np.concatenate([cos_a, -sin_a], axis=0)), axis=1))
        last.append(three_parts(np.concatenate([cos_a.T, -sin_a.T], axis=1) / seq, 1))
    turns = [np.concatenate(turn((4 * (k1 + m * rows) + 1) * r[None, :], 4 * seq), axis=1) for m in range(2)]
    cos_r, sin_r = turn(r[:, None] * r[None, :], LANES)
    forth = np.block([[cos_r, -sin_r], [sin_r, cos_r]])
    back = np.block([[cos_r, sin_r], [-sin_r, cos_r]])
    return (
        np.concatenate(first, axis=0),
        np.concatenate(last, axis=0),
        three_parts(forth, 0),
        three_parts(back, 0),
        np.concatenate(turns, axis=0).astype(np.float32),
    )


def dot(left, right):
    return jnp.dot(left, right, preferred_element_type=F32)


def split(value):
    high = value.astype(BF16)
    return high, (value - high.astype(F32)).astype(BF16)


def stack(value, axis):
    high, low = split(value)
    return jnp.concatenate([high, low, high], axis=axis)


def interleave(tasks, at_once):
    waiting, active = list(tasks), []
    while waiting or active:
        while waiting and len(active) < at_once:
            active.append(waiting.pop(0))
        for task in list(active):
            if next(task, "over") == "over":
                active.remove(task)


def word(code, exponent):
    negative = code >= 128.0
    size = jnp.where(negative, code, code + 128.0) * (1 / 128) * jnp.exp2(exponent)
    return jnp.where(negative, -size, size)


def code_of(held_word):
    size = jnp.abs(held_word)
    exponent = jnp.floor(jnp.log2(size) + 0.002)
    digits = jnp.floor(size * jnp.exp2(7.0 - exponent) + 0.5)
    return jnp.where(held_word < 0.0, digits, digits - 128.0), exponent


def encode(one, two):
    top = jnp.maximum(jnp.maximum(jnp.abs(one), jnp.abs(two)), 2.0**-115)
    exponent = jnp.floor(jnp.log2(top))
    scale = jnp.exp2(-exponent)
    one_code = jnp.floor(one * scale * STEPS + (2 * STEPS + 0.5))
    two_code = jnp.floor(two * scale * STEPS + (2 * STEPS + 0.5))
    coarse = jnp.floor(one_code * (1 / 16))
    rest = two_code * 16.0 + (one_code - 16.0 * coarse)
    upper = jnp.floor(rest * (1 / 256))
    return word(coarse, exponent), word(rest - 256.0 * upper, upper - 120.0)


def decode(first_word, second_word):
    coarse, exponent = code_of(first_word)
    lower, upper = code_of(second_word)
    rest = (upper + 120.0) * 256.0 + lower
    two_code = jnp.floor(rest * (1 / 16))
    one_code = 16.0 * coarse + (rest - 16.0 * two_code)
    scale = jnp.exp2(exponent) * (1 / STEPS)
    return (one_code - 2 * STEPS) * scale, (two_code - 2 * STEPS) * scale


def pack_kernel(peers, u_ref, g_ref, h_ref, out_ref, landed, taps_landed, held, sems):
    share = taps_landed.shape[0]
    own = pl.multiple_of(lax.axis_index("dp") * share, share)
    arrivals = (
        (pltpu.make_async_copy(h_ref.at[pl.ds(own, share), :], taps_landed, sems.at[2]), taps_landed, 32),
        (pltpu.make_async_copy(u_ref, landed.at[0], sems.at[0]), landed.at[0], 0),
        (pltpu.make_async_copy(g_ref, landed.at[1], sems.at[1]), landed.at[1], 16),
    )
    for copy, _, _ in arrivals:
        copy.start()
    for copy, block, first_row in arrivals:
        copy.wait()
        for q in range(block.shape[0] // LANES):
            flipped = block[q * LANES : (q + 1) * LANES, :].astype(F32).T
            for c in range(OWN):
                row = first_row + OWN * q + c
                held[pl.ds(row, peers, stride=40), :] = flipped[c * peers : (c + 1) * peers, :]
    out_ref[...] = held[0 : peers * 40, :].reshape(peers, 40, LANES).astype(BF16)


def unpack_kernel(peers, in_ref, input_ref, filter_ref, held, input_block, filter_block, sems):
    blocks = input_ref.shape[0] // LANES
    held[0 : peers * 24, :] = in_ref[...].astype(F32).reshape(peers * 24, LANES)
    leaving = []
    for q in range(blocks):
        rows = slice(q * LANES, (q + 1) * LANES)
        words = [held[pl.ds(16 + 2 * q + c, peers, stride=24), :] for c in range(2)]
        for c, piece in enumerate(decode(*words)):
            filter_block[rows, c * peers : (c + 1) * peers] = piece.T
        leaving.append(pltpu.make_async_copy(filter_block.at[rows], filter_ref.at[rows], sems.at[q]))
        leaving[-1].start()
    for q in range(blocks):
        rows = slice(q * LANES, (q + 1) * LANES)
        for c in range(OWN):
            piece = held[pl.ds(OWN * q + c, peers, stride=24), :]
            input_block[rows, c * peers : (c + 1) * peers] = piece.T.astype(BF16)
        leaving.append(pltpu.make_async_copy(input_block.at[rows], input_ref.at[rows], sems.at[blocks + q]))
        leaving[-1].start()
    for copy in leaving:
        copy.wait()


def convolve_kernel(group, in_ref, first_ref, last_ref, forth_ref, back_ref, turn_ref, out_ref, u_held, g_held, h_held, in_grad, taps_grad):
    rows = 2 * group
    for b in range(BATCH):
        got = in_ref[b * group : (b + 1) * group].astype(F32)
        u_held[b, 0 : group * 16, :] = got[:, 0:16].reshape(group * 16, LANES)
        g_held[b, 0 : group * 16, :] = got[:, 16:32].reshape(group * 16, LANES)
    taps = [in_ref[b * group : (b + 1) * group].astype(F32)[:, 32:40] for b in range(BATCH)]
    h_held[0, 0 : group * 16, :] = jnp.concatenate(taps, axis=1).reshape(group * 16, LANES)

    def columns(value):
        return value[:, :LANES], value[:, LANES:]

    def turns(m):
        return columns(turn_ref[m * rows : (m + 1) * rows, :])

    spectra = {}

    def forward(name, held, b, channels):
        both = []
        for q in range(2):
            values = jnp.concatenate(
                [held[b, pl.ds(OWN * q + c, rows, stride=2 * OWN), :].astype(BF16) for c in channels], axis=1
            )
            both.append(dot(first_ref[2 * rows * q : 2 * rows * (q + 1), :], jnp.concatenate([values, values], axis=0)))
        yield
        sums = (both[0] + both[1], both[0] - both[1])
        turned = []
        for i, c in enumerate(channels):
            for m in range(2):
                turn_cos, turn_sin = turns(m)
                real, imag = columns(sums[m][0:rows])[i], columns(sums[m][rows : 2 * rows])[i]
                turned.append(jnp.concatenate([real * turn_cos + imag * turn_sin, imag * turn_cos - real * turn_sin], axis=1))
        done = dot(stack(jnp.concatenate(turned, axis=0), 1), forth_ref[...])
        for i, c in enumerate(channels):
            spectra[name, c] = done[2 * rows * i : 2 * rows * (i + 1)]
        yield

    def correlate(left, right, c):
        left_re, left_im = columns(spectra[left, c])
        right_re, right_im = columns(spectra[right, c])
        return jnp.concatenate(
            [left_re * right_re + left_im * right_im, left_im * right_re - left_re * right_im], axis=1
        )

    def backward(pairs, channels, store):
        while not all((name, c) in spectra for pair in pairs for name in pair for c in channels):
            yield
        spread = []
        for c in channels:
            product = functools.reduce(jnp.add, [correlate(left, right, c) for left, right in pairs])
            spread.append(dot(stack(product, 1), back_ref[...]))
            yield
        yield
        terms = []
        for one in spread:
            for m in range(2):
                turn_cos, turn_sin = turns(m)
                real, imag = columns(one[m * rows : (m + 1) * rows])
                terms.append(jnp.concatenate([real * turn_cos - imag * turn_sin, imag * turn_cos + real * turn_sin], axis=0))
        results = []
        for q in range(2):
            turned = jnp.concatenate([terms[2 * i] + terms[2 * i + 1] if q == 0 else terms[2 * i] - terms[2 * i + 1] for i in range(2)], axis=1)
            results.append(dot(last_ref[rows * q : rows * (q + 1), :], stack(turned, 0)))
            yield
        yield
        store(results, channels)

    def store_input(b):
        def store(results, channels):
            for q in range(2):
                for i, c in enumerate(channels):
                    in_grad[b, pl.ds(OWN * q + c, rows, stride=2 * OWN), :] = columns(results[q])[i]

        return store

    def store_taps(results, channels):
        for q in range(2):
            for i, coded in enumerate(encode(*columns(results[q]))):
                taps_grad[channels[0] // 2, pl.ds(2 * q + i, rows, stride=4), :] = coded

    def forwards(names, half):
        held = {"g0": (g_held, 0), "g1": (g_held, 1), "h": (h_held, 0), "u0": (u_held, 0), "u1": (u_held, 1)}
        return [forward(name, *held[name], (2 * half, 2 * half + 1)) for name in names]

    def inputs(half):
        return [backward([(f"g{b}", "h")], (2 * half, 2 * half + 1), store_input(b)) for b in range(BATCH)]

    def taps_of(half):
        return [backward([("g0", "u0"), ("g1", "u1")], (2 * half, 2 * half + 1), store_taps)]

    later, ready = forwards(("u0", "u1", "g0", "g1", "h"), 1), inputs(0) + taps_of(0)
    tasks = forwards(("g0", "g1", "h", "u0", "u1"), 0)
    tasks += [later[0], ready[0], later[1], ready[1], later[2], later[3], ready[2], later[4]]
    tasks += taps_of(1) + inputs(1)
    interleave(tasks, 5)
    for d in range(2):
        out_ref[d * group : (d + 1) * group] = jnp.concatenate(
            [in_grad[d, 0 : group * 16, :].reshape(group, 16, LANES), taps_grad[d, 0 : group * 8, :].reshape(group, 8, LANES)], axis=1
        ).astype(BF16)


def shards(saved_input, output_grad, filter_taps):
    group = lax.axis_size("ctx")
    peers = 2 * group
    local_len, chan_count = filter_taps.shape
    seq = group * local_len
    constants = [jnp.asarray(table) for table in tables(seq)]
    params = pltpu.CompilerParams(vmem_limit_bytes=48 * 1024 * 1024)
    local = pl.BlockSpec(memory_space=pltpu.VMEM)
    far = pl.BlockSpec(memory_space=pltpu.HBM)
    packed = pl.pallas_call(
        functools.partial(pack_kernel, peers),
        out_shape=jax.ShapeDtypeStruct((peers, 40, LANES), BF16),
        in_specs=[far] * 3,
        out_specs=local,
        scratch_shapes=[
            pltpu.VMEM((2, local_len, chan_count), BF16),
            pltpu.VMEM((local_len // 2, chan_count), BF16),
            pltpu.VMEM(((peers + 1) * 40, LANES), F32),
            pltpu.SemaphoreType.DMA((3,)),
        ],
        compiler_params=params,
        name="pack",
    )(*[pltpu.with_memory_space_constraint(x, pltpu.HBM) for x in (saved_input[0], output_grad[0], filter_taps)])
    received = lax.all_to_all(packed, ("dp", "ctx"), split_axis=0, concat_axis=0, tiled=True)
    results = pl.pallas_call(
        functools.partial(convolve_kernel, group),
        out_shape=jax.ShapeDtypeStruct((peers, 24, LANES), BF16),
        scratch_shapes=[
            pltpu.VMEM((BATCH, group * 16 + 8, LANES), F32),
            pltpu.VMEM((BATCH, group * 16 + 8, LANES), F32),
            pltpu.VMEM((1, group * 16 + 8, LANES), F32),
            pltpu.VMEM((BATCH, group * 16 + 8, LANES), F32),
            pltpu.VMEM((BATCH, group * 8 + 8, LANES), F32),
        ],
        compiler_params=params,
        name="convolve",
    )(received, *constants)
    returned = lax.all_to_all(results, ("dp", "ctx"), split_axis=0, concat_axis=0, tiled=True)
    input_grad, filter_grad = pl.pallas_call(
        functools.partial(unpack_kernel, peers),
        out_shape=(
            jax.ShapeDtypeStruct((local_len, chan_count), BF16),
            jax.ShapeDtypeStruct((local_len, chan_count // 2), F32),
        ),
        in_specs=[local],
        out_specs=(far, far),
        scratch_shapes=[
            pltpu.VMEM(((peers + 1) * 24, LANES), F32),
            pltpu.VMEM((local_len, chan_count), BF16),
            pltpu.VMEM((local_len, chan_count // 2), F32),
            pltpu.SemaphoreType.DMA((2 * (local_len // LANES),)),
        ],
        compiler_params=params,
        name="unpack",
    )(returned)
    return input_grad[None], filter_grad


def solution(mesh):
    placed = (P("dp", "ctx", None), P("dp", "ctx", None), P("ctx", None))
    return jax.shard_map(
        shards,
        mesh=mesh,
        in_specs=placed,
        out_specs=(P("dp", "ctx", None), P("ctx", "dp")),
        check_vma=False,
    )
```

```python
import functools
import math

import jax
import jax.numpy as jnp
import ml_dtypes
import numpy as np
from jax import lax
from jax.experimental import pallas as pl
from jax.experimental.pallas import tpu as pltpu
from jax.sharding import PartitionSpec as P

LANES = 128
BF16 = jnp.bfloat16
F32 = jnp.float32
OWN = 4
BATCH = 2
STEPS = 959.0


def two_parts(matrix):
    high = matrix.astype(ml_dtypes.bfloat16)
    low = (matrix - high.astype(np.float64)).astype(ml_dtypes.bfloat16)
    return high, low


def three_parts(matrix, axis):
    high, low = two_parts(matrix)
    return np.concatenate([high, high, low], axis=axis)


def turn(numerator, period):
    phase = (numerator % period) * (2.0 * math.pi / period)
    return np.cos(phase), np.sin(phase)


@functools.cache
def tables(seq):
    rows = seq // (2 * LANES)
    k1 = np.arange(rows, dtype=np.int64)[:, None]
    a = np.arange(rows, dtype=np.int64)[None, :]
    r = np.arange(LANES, dtype=np.int64)
    first, last = [], []
    for q in range(2):
        cos_a, sin_a = turn((4 * k1 + 1) * (2 * a + q), 8 * rows)
        first.append(np.concatenate(two_parts(np.concatenate([cos_a, -sin_a], axis=0)), axis=1))
        last.append(three_parts(np.concatenate([cos_a.T, -sin_a.T], axis=1) / seq, 1))
    turns = [np.concatenate(turn((4 * (k1 + m * rows) + 1) * r[None, :], 4 * seq), axis=1) for m in range(2)]
    cos_r, sin_r = turn(r[:, None] * r[None, :], LANES)
    forth = np.block([[cos_r, -sin_r], [sin_r, cos_r]])
    back = np.block([[cos_r, sin_r], [-sin_r, cos_r]])
    return (
        np.concatenate(first, axis=0),
        np.concatenate(last, axis=0),
        three_parts(forth, 0),
        three_parts(back, 0),
        np.concatenate(turns, axis=0).astype(np.float32),
    )


def dot(left, right):
    return jnp.dot(left, right, preferred_element_type=F32)


def split(value):
    high = value.astype(BF16)
    return high, (value - high.astype(F32)).astype(BF16)


def stack(value, axis):
    high, low = split(value)
    return jnp.concatenate([high, low, high], axis=axis)


def interleave(tasks, at_once):
    waiting, active = list(tasks), []
    while waiting or active:
        while waiting and len(active) < at_once:
            active.append(waiting.pop(0))
        for task in list(active):
            if next(task, "over") == "over":
                active.remove(task)


def word(code, exponent):
    negative = code >= 128.0
    size = jnp.where(negative, code, code + 128.0) * (1 / 128) * jnp.exp2(exponent)
    return jnp.where(negative, -size, size)


def code_of(held_word):
    size = jnp.abs(held_word)
    exponent = jnp.floor(jnp.log2(size) + 0.002)
    digits = jnp.floor(size * jnp.exp2(7.0 - exponent) + 0.5)
    return jnp.where(held_word < 0.0, digits, digits - 128.0), exponent


def encode(one, two):
    top = jnp.maximum(jnp.maximum(jnp.abs(one), jnp.abs(two)), 2.0**-115)
    exponent = jnp.floor(jnp.log2(top))
    scale = jnp.exp2(-exponent)
    one_code = jnp.floor(one * scale * STEPS + (2 * STEPS + 0.5))
    two_code = jnp.floor(two * scale * STEPS + (2 * STEPS + 0.5))
    coarse = jnp.floor(one_code * (1 / 16))
    rest = two_code * 16.0 + (one_code - 16.0 * coarse)
    upper = jnp.floor(rest * (1 / 256))
    return word(coarse, exponent), word(rest - 256.0 * upper, upper - 120.0)


def decode(first_word, second_word):
    coarse, exponent = code_of(first_word)
    lower, upper = code_of(second_word)
    rest = (upper + 120.0) * 256.0 + lower
    two_code = jnp.floor(rest * (1 / 16))
    one_code = 16.0 * coarse + (rest - 16.0 * two_code)
    scale = jnp.exp2(exponent) * (1 / STEPS)
    return (one_code - 2 * STEPS) * scale, (two_code - 2 * STEPS) * scale


def pack_kernel(peers, u_ref, g_ref, h_ref, out_ref, landed, taps_landed, held, sems):
    share = taps_landed.shape[0]
    own = pl.multiple_of(lax.axis_index("dp") * share, share)
    arrivals = (
        (pltpu.make_async_copy(h_ref.at[pl.ds(own, share), :], taps_landed, sems.at[2]), taps_landed, 32),
        (pltpu.make_async_copy(u_ref, landed.at[0], sems.at[0]), landed.at[0], 0),
        (pltpu.make_async_copy(g_ref, landed.at[1], sems.at[1]), landed.at[1], 16),
    )
    for copy, _, _ in arrivals:
        copy.start()
    for copy, block, first_row in arrivals:
        copy.wait()
        for q in range(block.shape[0] // LANES):
            flipped = block[q * LANES : (q + 1) * LANES, :].astype(F32).T
            for c in range(OWN):
                row = first_row + OWN * q + c
                held[pl.ds(row, peers, stride=40), :] = flipped[c * peers : (c + 1) * peers, :]
    out_ref[...] = held[0 : peers * 40, :].reshape(peers, 40, LANES).astype(BF16)


def unpack_kernel(peers, in_ref, input_ref, filter_ref, held, input_block, filter_block, sems):
    blocks = input_ref.shape[0] // LANES
    held[0 : peers * 24, :] = in_ref[...].astype(F32).reshape(peers * 24, LANES)
    leaving = []
    for q in range(blocks):
        rows = slice(q * LANES, (q + 1) * LANES)
        words = [held[pl.ds(16 + 2 * q + c, peers, stride=24), :] for c in range(2)]
        for c, piece in enumerate(decode(*words)):
            filter_block[rows, c * peers : (c + 1) * peers] = piece.T
        leaving.append(pltpu.make_async_copy(filter_block.at[rows], filter_ref.at[rows], sems.at[q]))
        leaving[-1].start()
    for q in range(blocks):
        rows = slice(q * LANES, (q + 1) * LANES)
        for c in range(OWN):
            piece = held[pl.ds(OWN * q + c, peers, stride=24), :]
            input_block[rows, c * peers : (c + 1) * peers] = piece.T.astype(BF16)
        leaving.append(pltpu.make_async_copy(input_block.at[rows], input_ref.at[rows], sems.at[blocks + q]))
        leaving[-1].start()
    for copy in leaving:
        copy.wait()


def convolve_kernel(group, in_ref, first_ref, last_ref, forth_ref, back_ref, turn_ref, out_ref, u_held, g_held, h_held, in_grad, taps_grad):
    rows = 2 * group
    for b in range(BATCH):
        got = in_ref[b * group : (b + 1) * group].astype(F32)
        u_held[b, 0 : group * 16, :] = got[:, 0:16].reshape(group * 16, LANES)
        g_held[b, 0 : group * 16, :] = got[:, 16:32].reshape(group * 16, LANES)
    taps = [in_ref[b * group : (b + 1) * group].astype(F32)[:, 32:40] for b in range(BATCH)]
    h_held[0, 0 : group * 16, :] = jnp.concatenate(taps, axis=1).reshape(group * 16, LANES)

    def columns(value):
        return value[:, :LANES], value[:, LANES:]

    def turns(m):
        return columns(turn_ref[m * rows : (m + 1) * rows, :])

    spectra = {}

    def forward(name, held, b, channels):
        both = []
        for q in range(2):
            values = jnp.concatenate(
                [held[b, pl.ds(OWN * q + c, rows, stride=2 * OWN), :].astype(BF16) for c in channels], axis=1
            )
            both.append(dot(first_ref[2 * rows * q : 2 * rows * (q + 1), :], jnp.concatenate([values, values], axis=0)))
        yield
        sums = (both[0] + both[1], both[0] - both[1])
        turned = []
        for i, c in enumerate(channels):
            for m in range(2):
                turn_cos, turn_sin = turns(m)
                real, imag = columns(sums[m][0:rows])[i], columns(sums[m][rows : 2 * rows])[i]
                turned.append(jnp.concatenate([real * turn_cos + imag * turn_sin, imag * turn_cos - real * turn_sin], axis=1))
        done = dot(stack(jnp.concatenate(turned, axis=0), 1), forth_ref[...])
        for i, c in enumerate(channels):
            spectra[name, c] = done[2 * rows * i : 2 * rows * (i + 1)]
        yield

    def correlate(left, right, c):
        left_re, left_im = columns(spectra[left, c])
        right_re, right_im = columns(spectra[right, c])
        return jnp.concatenate(
            [left_re * right_re + left_im * right_im, left_im * right_re - left_re * right_im], axis=1
        )

    def backward(pairs, channels, store):
        while not all((name, c) in spectra for pair in pairs for name in pair for c in channels):
            yield
        spread = []
        for c in channels:
            product = functools.reduce(jnp.add, [correlate(left, right, c) for left, right in pairs])
            spread.append(dot(stack(product, 1), back_ref[...]))
            yield
        yield
        terms = []
        for one in spread:
            for m in range(2):
                turn_cos, turn_sin = turns(m)
                real, imag = columns(one[m * rows : (m + 1) * rows])
                terms.append(jnp.concatenate([real * turn_cos - imag * turn_sin, imag * turn_cos + real * turn_sin], axis=0))
        results = []
        for q in range(2):
            turned = jnp.concatenate([terms[2 * i] + terms[2 * i + 1] if q == 0 else terms[2 * i] - terms[2 * i + 1] for i in range(2)], axis=1)
            results.append(dot(last_ref[rows * q : rows * (q + 1), :], stack(turned, 0)))
            yield
        yield
        store(results, channels)

    def store_input(b):
        def store(results, channels):
            for q in range(2):
                for i, c in enumerate(channels):
                    in_grad[b, pl.ds(OWN * q + c, rows, stride=2 * OWN), :] = columns(results[q])[i]

        return store

    def store_taps(results, channels):
        for q in range(2):
            for i, coded in enumerate(encode(*columns(results[q]))):
                taps_grad[channels[0] // 2, pl.ds(2 * q + i, rows, stride=4), :] = coded

    def forwards(names, half):
        held = {"g0": (g_held, 0), "g1": (g_held, 1), "h": (h_held, 0), "u0": (u_held, 0), "u1": (u_held, 1)}
        return [forward(name, *held[name], (2 * half, 2 * half + 1)) for name in names]

    def inputs(half):
        return [backward([(f"g{b}", "h")], (2 * half, 2 * half + 1), store_input(b)) for b in range(BATCH)]

    def taps_of(half):
        return [backward([("g0", "u0"), ("g1", "u1")], (2 * half, 2 * half + 1), store_taps)]

    later, ready = forwards(('h', 'u0', 'u1', 'g0', 'g1'), 1), inputs(0) + taps_of(0)
    tasks = forwards(('g0', 'g1', 'h', 'u0', 'u1'), 0)
    tasks += [later[0], ready[0], later[1], ready[1], later[2], ready[2], later[3], later[4]]
    tasks += inputs(1) + taps_of(1)
    interleave(tasks, 5)
    for d in range(2):
        out_ref[d * group : (d + 1) * group] = jnp.concatenate(
            [in_grad[d, 0 : group * 16, :].reshape(group, 16, LANES), taps_grad[d, 0 : group * 8, :].reshape(group, 8, LANES)], axis=1
        ).astype(BF16)


def shards(saved_input, output_grad, filter_taps):
    group = lax.axis_size("ctx")
    peers = 2 * group
    local_len, chan_count = filter_taps.shape
    seq = group * local_len
    constants = [jnp.asarray(table) for table in tables(seq)]
    params = pltpu.CompilerParams(vmem_limit_bytes=48 * 1024 * 1024)
    local = pl.BlockSpec(memory_space=pltpu.VMEM)
    far = pl.BlockSpec(memory_space=pltpu.HBM)
    packed = pl.pallas_call(
        functools.partial(pack_kernel, peers),
        out_shape=jax.ShapeDtypeStruct((peers, 40, LANES), BF16),
        in_specs=[far] * 3,
        out_specs=local,
        scratch_shapes=[
            pltpu.VMEM((2, local_len, chan_count), BF16),
            pltpu.VMEM((local_len // 2, chan_count), BF16),
            pltpu.VMEM(((peers + 1) * 40, LANES), F32),
            pltpu.SemaphoreType.DMA((3,)),
        ],
        compiler_params=params,
        name="pack",
    )(*[pltpu.with_memory_space_constraint(x, pltpu.HBM) for x in (saved_input[0], output_grad[0], filter_taps)])
    received = lax.all_to_all(packed, ("dp", "ctx"), split_axis=0, concat_axis=0, tiled=True)
    results = pl.pallas_call(
        functools.partial(convolve_kernel, group),
        out_shape=jax.ShapeDtypeStruct((peers, 24, LANES), BF16),
        scratch_shapes=[
            pltpu.VMEM((BATCH, group * 16 + 8, LANES), F32),
            pltpu.VMEM((BATCH, group * 16 + 8, LANES), F32),
            pltpu.VMEM((1, group * 16 + 8, LANES), F32),
            pltpu.VMEM((BATCH, group * 16 + 8, LANES), F32),
            pltpu.VMEM((BATCH, group * 8 + 8, LANES), F32),
        ],
        compiler_params=params,
        name="convolve",
    )(received, *constants)
    returned = lax.all_to_all(results, ("dp", "ctx"), split_axis=0, concat_axis=0, tiled=True)
    input_grad, filter_grad = pl.pallas_call(
        functools.partial(unpack_kernel, peers),
        out_shape=(
            jax.ShapeDtypeStruct((local_len, chan_count), BF16),
            jax.ShapeDtypeStruct((local_len, chan_count // 2), F32),
        ),
        in_specs=[local],
        out_specs=(far, far),
        scratch_shapes=[
            pltpu.VMEM(((peers + 1) * 24, LANES), F32),
            pltpu.VMEM((local_len, chan_count), BF16),
            pltpu.VMEM((local_len, chan_count // 2), F32),
            pltpu.SemaphoreType.DMA((2 * (local_len // LANES),)),
        ],
        compiler_params=params,
        name="unpack",
    )(returned)
    return input_grad[None], filter_grad


def solution(mesh):
    placed = (P("dp", "ctx", None), P("dp", "ctx", None), P("ctx", None))
    return jax.shard_map(
        shards,
        mesh=mesh,
        in_specs=placed,
        out_specs=(P("dp", "ctx", None), P("ctx", "dp")),
        check_vma=False,
    )
```

```python
import functools
import math

import jax
import jax.numpy as jnp
import ml_dtypes
import numpy as np
from jax import lax
from jax.experimental import pallas as pl
from jax.experimental.pallas import tpu as pltpu
from jax.sharding import PartitionSpec as P

LANES = 128
BF16 = jnp.bfloat16
F32 = jnp.float32
OWN = 4
BATCH = 2
STEPS = 959.0


def two_parts(matrix):
    high = matrix.astype(ml_dtypes.bfloat16)
    low = (matrix - high.astype(np.float64)).astype(ml_dtypes.bfloat16)
    return high, low


def three_parts(matrix, axis):
    high, low = two_parts(matrix)
    return np.concatenate([high, high, low], axis=axis)


def turn(numerator, period):
    phase = (numerator % period) * (2.0 * math.pi / period)
    return np.cos(phase), np.sin(phase)


@functools.cache
def tables(seq):
    rows = seq // (2 * LANES)
    k1 = np.arange(rows, dtype=np.int64)[:, None]
    a = np.arange(rows, dtype=np.int64)[None, :]
    r = np.arange(LANES, dtype=np.int64)
    first, last = [], []
    for q in range(2):
        cos_a, sin_a = turn((4 * k1 + 1) * (2 * a + q), 8 * rows)
        first.append(np.concatenate(two_parts(np.concatenate([cos_a, -sin_a], axis=0)), axis=1))
        last.append(three_parts(np.concatenate([cos_a.T, -sin_a.T], axis=1) / seq, 1))
    turns = [np.concatenate(turn((4 * (k1 + m * rows) + 1) * r[None, :], 4 * seq), axis=1) for m in range(2)]
    cos_r, sin_r = turn(r[:, None] * r[None, :], LANES)
    forth = np.block([[cos_r, -sin_r], [sin_r, cos_r]])
    back = np.block([[cos_r, sin_r], [-sin_r, cos_r]])
    return (
        np.concatenate(first, axis=0),
        np.concatenate(last, axis=0),
        three_parts(forth, 0),
        three_parts(back, 0),
        np.concatenate(turns, axis=0).astype(np.float32),
    )


def dot(left, right):
    return jnp.dot(left, right, preferred_element_type=F32)


def split(value):
    high = value.astype(BF16)
    return high, (value - high.astype(F32)).astype(BF16)


def stack(value, axis):
    high, low = split(value)
    return jnp.concatenate([high, low, high], axis=axis)


def interleave(tasks, at_once):
    waiting, active = list(tasks), []
    while waiting or active:
        while waiting and len(active) < at_once:
            active.append(waiting.pop(0))
        for task in list(active):
            if next(task, "over") == "over":
                active.remove(task)


def word(code, exponent):
    negative = code >= 128.0
    size = jnp.where(negative, code, code + 128.0) * (1 / 128) * jnp.exp2(exponent)
    return jnp.where(negative, -size, size)


def code_of(held_word):
    size = jnp.abs(held_word)
    exponent = jnp.floor(jnp.log2(size) + 0.002)
    digits = jnp.floor(size * jnp.exp2(7.0 - exponent) + 0.5)
    return jnp.where(held_word < 0.0, digits, digits - 128.0), exponent


def encode(one, two):
    top = jnp.maximum(jnp.maximum(jnp.abs(one), jnp.abs(two)), 2.0**-115)
    exponent = jnp.floor(jnp.log2(top))
    scale = jnp.exp2(-exponent)
    one_code = jnp.floor(one * scale * STEPS + (2 * STEPS + 0.5))
    two_code = jnp.floor(two * scale * STEPS + (2 * STEPS + 0.5))
    coarse = jnp.floor(one_code * (1 / 16))
    rest = two_code * 16.0 + (one_code - 16.0 * coarse)
    upper = jnp.floor(rest * (1 / 256))
    return word(coarse, exponent), word(rest - 256.0 * upper, upper - 120.0)


def decode(first_word, second_word):
    coarse, exponent = code_of(first_word)
    lower, upper = code_of(second_word)
    rest = (upper + 120.0) * 256.0 + lower
    two_code = jnp.floor(rest * (1 / 16))
    one_code = 16.0 * coarse + (rest - 16.0 * two_code)
    scale = jnp.exp2(exponent) * (1 / STEPS)
    return (one_code - 2 * STEPS) * scale, (two_code - 2 * STEPS) * scale


def pack_kernel(peers, u_ref, g_ref, h_ref, out_ref, landed, taps_landed, held, sems):
    share = taps_landed.shape[0]
    own = pl.multiple_of(lax.axis_index("dp") * share, share)
    arrivals = (
        (pltpu.make_async_copy(h_ref.at[pl.ds(own, share), :], taps_landed, sems.at[2]), taps_landed, 32),
        (pltpu.make_async_copy(u_ref, landed.at[0], sems.at[0]), landed.at[0], 0),
        (pltpu.make_async_copy(g_ref, landed.at[1], sems.at[1]), landed.at[1], 16),
    )
    for copy, _, _ in arrivals:
        copy.start()
    for copy, block, first_row in arrivals:
        copy.wait()
        for q in range(block.shape[0] // LANES):
            flipped = block[q * LANES : (q + 1) * LANES, :].astype(F32).T
            for c in range(OWN):
                row = first_row + OWN * q + c
                held[pl.ds(row, peers, stride=40), :] = flipped[c * peers : (c + 1) * peers, :]
    out_ref[...] = held[0 : peers * 40, :].reshape(peers, 40, LANES).astype(BF16)


def unpack_kernel(peers, in_ref, input_ref, filter_ref, held, input_block, filter_block, sems):
    blocks = input_ref.shape[0] // LANES
    held[0 : peers * 24, :] = in_ref[...].astype(F32).reshape(peers * 24, LANES)
    leaving = []
    for q in range(blocks):
        rows = slice(q * LANES, (q + 1) * LANES)
        words = [held[pl.ds(16 + 2 * q + c, peers, stride=24), :] for c in range(2)]
        for c, piece in enumerate(decode(*words)):
            filter_block[rows, c * peers : (c + 1) * peers] = piece.T
        leaving.append(pltpu.make_async_copy(filter_block.at[rows], filter_ref.at[rows], sems.at[q]))
        leaving[-1].start()
    for q in range(blocks):
        rows = slice(q * LANES, (q + 1) * LANES)
        for c in range(OWN):
            piece = held[pl.ds(OWN * q + c, peers, stride=24), :]
            input_block[rows, c * peers : (c + 1) * peers] = piece.T.astype(BF16)
        leaving.append(pltpu.make_async_copy(input_block.at[rows], input_ref.at[rows], sems.at[blocks + q]))
        leaving[-1].start()
    for copy in leaving:
        copy.wait()


def convolve_kernel(group, in_ref, first_ref, last_ref, forth_ref, back_ref, turn_ref, out_ref, u_held, g_held, h_held, in_grad, taps_grad):
    rows = 2 * group
    arrived = set()

    def arrive(name):
        if name in arrived:
            return
        arrived.add(name)
        if name == "h":
            taps = [in_ref[b * group : (b + 1) * group].astype(F32)[:, 32:40] for b in range(BATCH)]
            h_held[0, 0 : group * 16, :] = jnp.concatenate(taps, axis=1).reshape(group * 16, LANES)
            return
        b, held, row = int(name[1]), u_held if name[0] == "u" else g_held, 0 if name[0] == "u" else 16
        got = in_ref[b * group : (b + 1) * group].astype(F32)
        held[b, 0 : group * 16, :] = got[:, row : row + 16].reshape(group * 16, LANES)

    def columns(value):
        return value[:, :LANES], value[:, LANES:]

    def turns(m):
        return columns(turn_ref[m * rows : (m + 1) * rows, :])

    spectra = {}

    def forward(name, held, b, channels):
        arrive(name)
        both = []
        for q in range(2):
            values = jnp.concatenate(
                [held[b, pl.ds(OWN * q + c, rows, stride=2 * OWN), :].astype(BF16) for c in channels], axis=1
            )
            both.append(dot(first_ref[2 * rows * q : 2 * rows * (q + 1), :], jnp.concatenate([values, values], axis=0)))
        yield
        sums = (both[0] + both[1], both[0] - both[1])
        turned = []
        for i, c in enumerate(channels):
            for m in range(2):
                turn_cos, turn_sin = turns(m)
                real, imag = columns(sums[m][0:rows])[i], columns(sums[m][rows : 2 * rows])[i]
                turned.append(jnp.concatenate([real * turn_cos + imag * turn_sin, imag * turn_cos - real * turn_sin], axis=1))
        done = dot(stack(jnp.concatenate(turned, axis=0), 1), forth_ref[...])
        for i, c in enumerate(channels):
            spectra[name, c] = done[2 * rows * i : 2 * rows * (i + 1)]
        yield

    def correlate(left, right, c):
        left_re, left_im = columns(spectra[left, c])
        right_re, right_im = columns(spectra[right, c])
        return jnp.concatenate(
            [left_re * right_re + left_im * right_im, left_im * right_re - left_re * right_im], axis=1
        )

    def backward(pairs, channels, store):
        while not all((name, c) in spectra for pair in pairs for name in pair for c in channels):
            yield
        spread = []
        for c in channels:
            product = functools.reduce(jnp.add, [correlate(left, right, c) for left, right in pairs])
            spread.append(dot(stack(product, 1), back_ref[...]))
            yield
        yield
        terms = []
        for one in spread:
            for m in range(2):
                turn_cos, turn_sin = turns(m)
                real, imag = columns(one[m * rows : (m + 1) * rows])
                terms.append(jnp.concatenate([real * turn_cos - imag * turn_sin, imag * turn_cos + real * turn_sin], axis=0))
        results = []
        for q in range(2):
            turned = jnp.concatenate([terms[2 * i] + terms[2 * i + 1] if q == 0 else terms[2 * i] - terms[2 * i + 1] for i in range(2)], axis=1)
            results.append(dot(last_ref[rows * q : rows * (q + 1), :], stack(turned, 0)))
            yield
        yield
        store(results, channels)

    def store_input(b):
        def store(results, channels):
            for q in range(2):
                for i, c in enumerate(channels):
                    in_grad[b, pl.ds(OWN * q + c, rows, stride=2 * OWN), :] = columns(results[q])[i]

        return store

    def store_taps(results, channels):
        for q in range(2):
            for i, coded in enumerate(encode(*columns(results[q]))):
                taps_grad[channels[0] // 2, pl.ds(2 * q + i, rows, stride=4), :] = coded

    def forwards(names, half):
        held = {"g0": (g_held, 0), "g1": (g_held, 1), "h": (h_held, 0), "u0": (u_held, 0), "u1": (u_held, 1)}
        return [forward(name, *held[name], (2 * half, 2 * half + 1)) for name in names]

    def inputs(half):
        return [backward([(f"g{b}", "h")], (2 * half, 2 * half + 1), store_input(b)) for b in range(BATCH)]

    def taps_of(half):
        return [backward([("g0", "u0"), ("g1", "u1")], (2 * half, 2 * half + 1), store_taps)]

    later, ready = forwards(('h', 'u0', 'u1', 'g0', 'g1'), 1), inputs(0) + taps_of(0)
    tasks = forwards(('g0', 'g1', 'h', 'u0', 'u1'), 0)
    tasks += [later[0], ready[0], later[1], ready[1], later[2], ready[2], later[3], later[4]]
    tasks += inputs(1) + taps_of(1)
    interleave(tasks, 5)
    for d in range(2):
        out_ref[d * group : (d + 1) * group] = jnp.concatenate(
            [in_grad[d, 0 : group * 16, :].reshape(group, 16, LANES), taps_grad[d, 0 : group * 8, :].reshape(group, 8, LANES)], axis=1
        ).astype(BF16)


def shards(saved_input, output_grad, filter_taps):
    group = lax.axis_size("ctx")
    peers = 2 * group
    local_len, chan_count = filter_taps.shape
    seq = group * local_len
    constants = [jnp.asarray(table) for table in tables(seq)]
    params = pltpu.CompilerParams(vmem_limit_bytes=48 * 1024 * 1024)
    local = pl.BlockSpec(memory_space=pltpu.VMEM)
    far = pl.BlockSpec(memory_space=pltpu.HBM)
    packed = pl.pallas_call(
        functools.partial(pack_kernel, peers),
        out_shape=jax.ShapeDtypeStruct((peers, 40, LANES), BF16),
        in_specs=[far] * 3,
        out_specs=local,
        scratch_shapes=[
            pltpu.VMEM((2, local_len, chan_count), BF16),
            pltpu.VMEM((local_len // 2, chan_count), BF16),
            pltpu.VMEM(((peers + 1) * 40, LANES), F32),
            pltpu.SemaphoreType.DMA((3,)),
        ],
        compiler_params=params,
        name="pack",
    )(*[pltpu.with_memory_space_constraint(x, pltpu.HBM) for x in (saved_input[0], output_grad[0], filter_taps)])
    received = lax.all_to_all(packed, ("dp", "ctx"), split_axis=0, concat_axis=0, tiled=True)
    results = pl.pallas_call(
        functools.partial(convolve_kernel, group),
        out_shape=jax.ShapeDtypeStruct((peers, 24, LANES), BF16),
        scratch_shapes=[
            pltpu.VMEM((BATCH, group * 16 + 8, LANES), F32),
            pltpu.VMEM((BATCH, group * 16 + 8, LANES), F32),
            pltpu.VMEM((1, group * 16 + 8, LANES), F32),
            pltpu.VMEM((BATCH, group * 16 + 8, LANES), F32),
            pltpu.VMEM((BATCH, group * 8 + 8, LANES), F32),
        ],
        compiler_params=params,
        name="convolve",
    )(received, *constants)
    returned = lax.all_to_all(results, ("dp", "ctx"), split_axis=0, concat_axis=0, tiled=True)
    input_grad, filter_grad = pl.pallas_call(
        functools.partial(unpack_kernel, peers),
        out_shape=(
            jax.ShapeDtypeStruct((local_len, chan_count), BF16),
            jax.ShapeDtypeStruct((local_len, chan_count // 2), F32),
        ),
        in_specs=[local],
        out_specs=(far, far),
        scratch_shapes=[
            pltpu.VMEM(((peers + 1) * 24, LANES), F32),
            pltpu.VMEM((local_len, chan_count), BF16),
            pltpu.VMEM((local_len, chan_count // 2), F32),
            pltpu.SemaphoreType.DMA((2 * (local_len // LANES),)),
        ],
        compiler_params=params,
        name="unpack",
    )(returned)
    return input_grad[None], filter_grad


def solution(mesh):
    placed = (P("dp", "ctx", None), P("dp", "ctx", None), P("ctx", None))
    return jax.shard_map(
        shards,
        mesh=mesh,
        in_specs=placed,
        out_specs=(P("dp", "ctx", None), P("ctx", "dp")),
        check_vma=False,
    )
```
